32 devices in a mesh: vocab: 8 (over z, x), tp: 4 (over y, core).
Axes of the slice: x: 2, y: 2, z: 4, core: 2. Of those that a mesh axis runs over, the one named last changes fastest.
Arguments:
- hidden: bfloat16 [4096, 2048], P('vocab'), may hold values from -28 to 28, as said below
- target_cluster: int32 [4096, 1], P('vocab'), may hold values from 0 to 63; in each aligned block of 512 rows (0 to 511, 512 to 1023, ...) at most 16 rows name the same one
- target_word: int32 [4096], P('vocab'), may hold values from 0 to 8191
- head_words: bfloat16 [2048, 8192], P(None, 'tp'), may hold values from -4 to 4
- head_clusters: bfloat16 [2048, 32], P(None, 'tp'), may hold values from -4 to 4
- proj_one: bfloat16 [8, 2048, 1024], P('vocab'), may hold values from -0.125 to 0.125
- proj_two: bfloat16 [8, 2048, 512], P('vocab'), may hold values from -0.125 to 0.125
- proj_three: bfloat16 [8, 2048, 256], P('vocab'), may hold values from -0.125 to 0.125
- proj_four: bfloat16 [8, 2048, 128], P('vocab'), may hold values from -0.125 to 0.125
- out_one: bfloat16 [8, 1024, 1024], P('vocab', None, 'tp'), may hold values from -4 to 4
- out_two: bfloat16 [8, 512, 2048], P('vocab', None, 'tp'), may hold values from -4 to 4
- out_three: bfloat16 [8, 256, 4096], P('vocab', None, 'tp'), may hold values from -4 to 4
- out_four: bfloat16 [8, 128, 8192], P('vocab', None, 'tp'), may hold values from -4 to 4
Outputs:
- grad_hidden: bfloat16 [4096, 2048], P('vocab', 'tp')
- grad_head_words: bfloat16 [2048, 8192], P('vocab', 'tp')
- grad_head_clusters: bfloat16 [2048, 32], P('vocab', 'tp')
- grad_proj_one: bfloat16 [8, 2048, 1024], P('vocab', 'tp')
- grad_proj_two: bfloat16 [8, 2048, 512], P('vocab', 'tp')
- grad_proj_three: bfloat16 [8, 2048, 256], P('vocab', 'tp')
- grad_proj_four: bfloat16 [8, 2048, 128], P('vocab', 'tp')
- grad_out_one: bfloat16 [8, 1024, 1024], P('vocab', None, 'tp')
- grad_out_two: bfloat16 [8, 512, 2048], P('vocab', None, 'tp')
- grad_out_three: bfloat16 [8, 256, 4096], P('vocab', None, 'tp')
- grad_out_four: bfloat16 [8, 128, 8192], P('vocab', None, 'tp')
The draws below stay inside these ranges and needn't reach their ends.
Inputs may be any that keep to these rules, and one draw needn't show every extreme that they name: `hidden`: real values of order one, up to a factor that differs between tokens. `target_cluster`: A value below 32 names the tail cluster of the token's word; 32 or more marks a word of the head. Among the 512 tokens of one index of vocab no tail cluster is named more than 16 times. `target_word`: for a tail token only the value modulo its cluster's vocabulary counts.
All inputs are finite; a program needn't handle non-finite values.
Results may differ from the reference program's by a relative error of at most 0.017.
Values may be sent and summed in bfloat16 or wider, within the bound.
No kernel may reach another device: no remote copies, remote signals or barrier semaphores. Data moves between devices by JAX's collectives and lax.ppermute only.
A program may use at most 128 MiB of HBM per device.

```python
import math
import jax
import jax.numpy as jnp
import numpy as np
from jax import lax

D = 2048
HEAD_WORDS = 8192
D1 = 1024
D2 = 512
D3 = 256
D4 = 128
VOC1 = 1024
VOC2 = 2048
VOC3 = 4096
VOC4 = 8192
TOK_DEV = 512
CL_BAND = 8
CLUSTERS = 32
CAP = 16
TOKENS = 4096
N_VOCAB = 8


def draw_hidden(key, part):
    first, second = jax.random.split(key)
    scales = jnp.exp(jax.random.uniform(second, (TOKENS, 1), jnp.float32, jnp.log(0.25), jnp.log(4.0)))
    values = jnp.clip(jax.random.normal(first, (TOKENS, D), jnp.float32), -6.0, 6.0) * scales
    return values.astype(jnp.bfloat16)


def head_offset(key):
    return jax.random.uniform(jax.random.fold_in(key, 7001), (D, 1), jnp.float32, -0.3, 0.3)


def band_offset(key, salt_value, width):
    return jax.random.uniform(jax.random.fold_in(key, salt_value), (CL_BAND, width, 1), jnp.float32, -0.3, 0.3)


def shifted(key, salt_value, shape, fan_in, offset):
    values = jnp.clip(jax.random.normal(jax.random.fold_in(key, salt_value), shape, jnp.float32), -3.0, 3.0)
    return values * (16.0 / fan_in) ** 0.5 + offset


def draw_head_words(key, part):
    return shifted(key, 7002, (D, HEAD_WORDS), D, head_offset(key)).astype(jnp.bfloat16)


def draw_head_clusters(key, part):
    return shifted(key, 7003, (D, CLUSTERS), D, head_offset(key)).astype(jnp.bfloat16)


def draw_out_one(key, part):
    return shifted(key, 7201, (CL_BAND, D1, VOC1), D1, band_offset(key, 7101, D1)).astype(jnp.bfloat16)


def draw_out_two(key, part):
    return shifted(key, 7202, (CL_BAND, D2, VOC2), D2, band_offset(key, 7102, D2)).astype(jnp.bfloat16)


def draw_out_three(key, part):
    return shifted(key, 7203, (CL_BAND, D3, VOC3), D3, band_offset(key, 7103, D3)).astype(jnp.bfloat16)


def draw_out_four(key, part):
    return shifted(key, 7204, (CL_BAND, D4, VOC4), D4, band_offset(key, 7104, D4)).astype(jnp.bfloat16)


def place_ends(drawn, rng, least, top_value):
    index_at = [jax.random.randint(jax.random.fold_in(rng, axis), (), 0, length) for axis, length in enumerate(drawn.shape)]
    widest = drawn.shape.index(max(drawn.shape))
    beside = index_at[:widest] + [(index_at[widest] + 1) % drawn.shape[widest]] + index_at[widest + 1:]
    return drawn.at[tuple(index_at)].set(least).at[tuple(beside)].set(top_value)


def levels(rng, dims, cuts, least, largest):
    def one(axis_at, blocks):
        heights = jax.random.uniform(jax.random.fold_in(jax.random.fold_in(rng, 6), axis_at), (blocks,), jnp.float32, least / len(cuts), largest / len(cuts))
        return jnp.repeat(jnp.exp(heights), dims[axis_at] // blocks).reshape((-1,) + (1,) * (len(dims) - axis_at - 1))

    level = one(*cuts[0])
    for cut in cuts[1:]:
        level = level * one(*cut)
    return level


def cumulative_ranks(count, slope):
    weights = [(1 << 20) // math.isqrt(rank ** slope) + 1 for rank in range(1, count + 1)]
    scale = 1 + sum(weights) // (1 << 30)
    return np.cumsum(np.array([max(1, weight // scale) for weight in weights]))


def ranked_ids(own_key, shape, count, skew):
    grid = cumulative_ranks(count, skew)
    ticket = jax.random.randint(jax.random.fold_in(own_key, 1), shape, 0, int(grid[count - 1]))
    grade = jnp.searchsorted(jnp.asarray(grid, jnp.int32), ticket, side="right")
    return jax.random.permutation(jax.random.fold_in(own_key, 2), count)[grade].astype(jnp.int32)


def routed_block(key, own, number, rows, number_of, top, most, slope):
    ranking = jax.random.permutation(key, number_of)
    packed, ordinary = load_shares(number_of, rows * top, most, slope, True), load_shares(number_of, rows * top, most, slope, False)
    places = jnp.arange(number_of)

    def named(tallies, offset_by):
        used = int((tallies > 0).sum())
        fixed = max(1, used // 4)
        passed = fixed + (places - fixed + offset_by * (used - fixed)) % max(1, number_of - fixed)
        return jnp.zeros((number_of,), jnp.int32).at[ranking[jnp.where(places < fixed, places, passed)]].set(jnp.asarray(tallies, jnp.int32))

    tallies = jnp.where(number % 4 == 0, named(packed, number // 4), named(ordinary, number - number // 4 - 1))
    mixed = jax.random.permutation(jax.random.fold_in(own, 3), number_of)
    giver, receiver = mixed[0:number_of // 2 * 2:2], mixed[1:number_of // 2 * 2:2]
    slack = jnp.minimum(tallies[giver] - 1, most - tallies[receiver]) // 2
    slack = jnp.where((giver == ranking[0]) | (receiver == ranking[0]) | (tallies[receiver] == 0), 0, jnp.maximum(slack, 0))
    passed = jax.random.randint(jax.random.fold_in(own, 4), (number_of // 2,), 0, 1 << 20) % (slack + 1)
    tallies = tallies.at[giver].add(-passed).at[receiver].add(passed)
    items = jnp.searchsorted(jnp.cumsum(tallies), jnp.arange(rows * top), side="right").astype(jnp.int32)
    grid = items.reshape(top, rows).T
    grid = grid[jax.random.permutation(jax.random.fold_in(own, 1), rows)]
    offset_by = jax.random.randint(jax.random.fold_in(own, 2), (rows, 1), 0, top)
    return jnp.take_along_axis(grid, (jnp.arange(top)[None, :] + offset_by) % top, axis=1)


def load_shares(count, total, most, skew, full):
    portions = [(1 << 20) // math.isqrt(grade ** skew) + 1 for grade in range(1, count + 1)]
    largest = most if full else min(most, max(-(-total // count), total * portions[0] // sum(portions)))
    least = 1 if total - largest >= count - 1 else 0
    given, surplus = [largest] + [least] * (count - 1), total - largest - least * (count - 1)
    while surplus > 0:
        free = [i for i in range(1, count) if given[i] < largest] or [i for i in range(1, count) if given[i] < most]
        pool, left = sum([portions[i] for i in free]), surplus
        for i in free:
            addition = min(most - given[i], max(1, left * portions[i] // pool), surplus)
            given[i] = given[i] + addition
            surplus = surplus - addition
    return np.array(given)


def noise(stream_key, extent, spread, limit, pieces=(), kind=jnp.bfloat16):
    entries = spread * jax.random.normal(stream_key, extent, jnp.float32)
    if pieces:
        entries = entries * levels(stream_key, extent, pieces, -0.22, 0.18)
    return jnp.clip(entries, -limit, limit).astype(kind)


def setup_inputs(seed: int = 0) -> dict:
    splits = jax.random.split(jax.random.key(seed), 14)
    hidden = draw_hidden(jax.random.fold_in(splits[13], 71), 0)
    target_cluster_keys = jax.random.split(jax.random.fold_in(splits[1], 1), TOKENS // TOK_DEV)
    target_cluster_turns = jax.random.permutation(jax.random.fold_in(splits[1], 3), TOKENS // TOK_DEV)
    target_cluster = jax.vmap(lambda own, number: routed_block(jax.random.fold_in(splits[1], 2), own, number, TOK_DEV, 2 * CLUSTERS, 1, CAP, 2))(target_cluster_keys, target_cluster_turns).reshape((TOKENS, 1))
    target_word = place_ends(ranked_ids(splits[2], (TOKENS,), HEAD_WORDS, 1), jax.random.fold_in(splits[2], 3), 0, HEAD_WORDS - 1).astype(jnp.int32)
    head_words = draw_head_words(jax.random.fold_in(splits[13], 71), 0)
    head_clusters = draw_head_clusters(jax.random.fold_in(splits[13], 71), 0)
    proj_one = noise(splits[5], (CL_BAND, D, D1), D ** -0.5, 0.125, ((0, 8),))
    proj_two = noise(splits[6], (CL_BAND, D, D2), D ** -0.5, 0.125, ((0, 8),))
    proj_three = noise(splits[7], (CL_BAND, D, D3), D ** -0.5, 0.125, ((0, 8),))
    proj_four = noise(splits[8], (CL_BAND, D, D4), D ** -0.5, 0.125, ((0, 8),))
    out_one = draw_out_one(jax.random.fold_in(splits[13], 71), 0)
    out_two = draw_out_two(jax.random.fold_in(splits[13], 71), 0)
    out_three = draw_out_three(jax.random.fold_in(splits[13], 71), 0)
    out_four = draw_out_four(jax.random.fold_in(splits[13], 71), 0)
    return {"hidden": hidden, "target_cluster": target_cluster, "target_word": target_word, "head_words": head_words, "head_clusters": head_clusters, "proj_one": proj_one, "proj_two": proj_two, "proj_three": proj_three, "proj_four": proj_four, "out_one": out_one, "out_two": out_two, "out_three": out_three, "out_four": out_four}


def head_pass(hidden, head_col, weights):
    cols = weights.shape[1]
    blocks_rows = hidden.reshape(-1, TOK_DEV, D)
    blocks_cols = head_col.reshape(-1, TOK_DEV)

    def step(carry, inputs):
        rows, target = inputs
        logits = jnp.dot(rows, weights, preferred_element_type=jnp.float32)
        peak = jnp.max(logits, axis=1, keepdims=True)
        expd = jnp.exp(logits - peak)
        probs = expd / jnp.sum(expd, axis=1, keepdims=True)
        hit = (jnp.arange(cols, dtype=jnp.int32)[None, :] == target[:, None]).astype(jnp.float32)
        grads = (probs - hit).astype(jnp.bfloat16)
        back = jnp.dot(grads, weights.T, preferred_element_type=jnp.float32)
        return carry + jnp.dot(rows.T, grads, preferred_element_type=jnp.float32), back

    init = jnp.zeros((D, cols), jnp.float32)
    total, backs = lax.scan(step, init, (blocks_rows, blocks_cols))
    return total, backs.reshape(-1, D)


def band_pass(rows, words, proj, outw, vocab):
    def one(args):
        block, word, weight_in, weight_out = args
        valid = word >= 0
        local = jnp.where(valid, word % vocab, -1)
        reduced = jnp.dot(block, weight_in, preferred_element_type=jnp.float32).astype(jnp.bfloat16)
        logits = jnp.dot(reduced, weight_out, preferred_element_type=jnp.float32)
        peak = jnp.max(logits, axis=1, keepdims=True)
        expd = jnp.exp(logits - peak)
        probs = expd / jnp.sum(expd, axis=1, keepdims=True)
        hit = (jnp.arange(vocab, dtype=jnp.int32)[None, :] == local[:, None]).astype(jnp.float32)
        dlog = ((probs - hit) * valid[:, None].astype(jnp.float32)).astype(jnp.bfloat16)
        dred = jnp.dot(dlog, weight_out.T, preferred_element_type=jnp.float32).astype(jnp.bfloat16)
        grad_out = jnp.dot(reduced.T, dlog, preferred_element_type=jnp.float32).astype(jnp.bfloat16)
        grad_proj = jnp.dot(block.T, dred, preferred_element_type=jnp.float32).astype(jnp.bfloat16)
        back = jnp.dot(dred, weight_in.T, preferred_element_type=jnp.float32).astype(jnp.bfloat16)
        return grad_out, grad_proj, back

    return lax.map(one, (rows, words, proj, outw))


def reference(hidden, target_cluster, target_word, head_words, head_clusters, proj_one, proj_two, proj_three, proj_four, out_one, out_two, out_three, out_four):
    clus = target_cluster[:, 0]
    tail = clus < CLUSTERS
    head_col = jnp.where(tail, HEAD_WORDS + clus, target_word).astype(jnp.int32)
    weights = jnp.concatenate([head_words, head_clusters], axis=1)
    head_total, head_back = head_pass(hidden, head_col, weights)

    tok_index = jnp.arange(TOKENS, dtype=jnp.int32)
    member = (clus.reshape(N_VOCAB, TOK_DEV)[:, :, None] == jnp.arange(CLUSTERS, dtype=jnp.int32)[None, None, :]).astype(jnp.int32)
    rank = jnp.sum((jnp.cumsum(member, axis=1) - 1) * member, axis=2).reshape(TOKENS)
    source = tok_index // TOK_DEV
    row_key = jnp.where(tail, clus, CLUSTERS).astype(jnp.int32)
    slot = (source * CAP + rank).astype(jnp.int32)
    table = jnp.full((CLUSTERS, N_VOCAB * CAP), TOKENS, jnp.int32).at[row_key, slot].set(tok_index, mode="drop")
    hidden_pad = jnp.concatenate([hidden, jnp.zeros((1, D), jnp.bfloat16)], axis=0)
    word_pad = jnp.concatenate([target_word, jnp.full((1,), -1, jnp.int32)], axis=0)

    tail_back = jnp.zeros((TOKENS + 1, D), jnp.float32)
    grads_out = []
    grads_proj = []
    bands = ((proj_one, out_one, VOC1), (proj_two, out_two, VOC2), (proj_three, out_three, VOC3), (proj_four, out_four, VOC4))
    for band, (proj, outw, vocab) in enumerate(bands):
        table_band = table[band * CL_BAND:(band + 1) * CL_BAND]
        rows = hidden_pad[table_band]
        words = word_pad[table_band]
        grad_out, grad_proj, back = band_pass(rows, words, proj, outw, vocab)
        tail_back = tail_back.at[table_band.reshape(-1)].add(back.reshape(-1, D).astype(jnp.float32))
        grads_out.append(grad_out)
        grads_proj.append(grad_proj)

    grad_hidden = (head_back + tail_back[:TOKENS]).astype(jnp.bfloat16)
    grad_head_words = head_total[:, :HEAD_WORDS].astype(jnp.bfloat16)
    grad_head_clusters = head_total[:, HEAD_WORDS:].astype(jnp.bfloat16)
    return (grad_hidden, grad_head_words, grad_head_clusters, grads_proj[0], grads_proj[1], grads_proj[2], grads_proj[3], grads_out[0], grads_out[1], grads_out[2], grads_out[3])
```

```python
import functools

import jax
import jax.numpy as jnp
from jax import lax
from jax.experimental import pallas as pl
from jax.experimental.pallas import tpu as pltpu
from jax.sharding import PartitionSpec as P

F32 = jnp.float32
BF16 = jnp.bfloat16
I32 = jnp.int32
LANES = 128


def xor_pairs(size, step):
    return [(i, i ^ step) for i in range(size)]


def tp_swap(value, step):
    return lax.ppermute(value, "tp", xor_pairs(lax.axis_size("tp"), step))


def dot_nn(a, b):
    return lax.dot_general(a, b, (((1,), (0,)), ((), ())), preferred_element_type=F32)


def dot_nt(a, b):
    return lax.dot_general(a, b, (((1,), (1,)), ((), ())), preferred_element_type=F32)


def dot_tn(a, b):
    return lax.dot_general(a, b, (((0,), (0,)), ((), ())), preferred_element_type=F32)


def struct(shape, dtype):
    return jax.ShapeDtypeStruct(shape, dtype)


def whole(array):
    rank = len(array.shape)
    return pl.BlockSpec(array.shape, lambda *_: (0,) * rank)


COST_SCALE = 1.0
MICROSECONDS = {
    "send_rows": 3,
    "head_logits": 9,
    "line_logits": 20,
    "head_back": 9,
    "head_weights": 8,
    "turned_rows": 2,
    "tail_logits": 5,
    "tail_grads": 3,
    "tail_back": 3,
    "add": 1,
    "grad_hidden": 2,
}


SMALL = ("add",)


def kernel_call(kernel, name, scalars, operands, in_specs, outs, out_specs, scratch=(), grid=(1,)):
    return pl.pallas_call(
        kernel,
        name=name,
        out_shape=outs,
        grid_spec=pltpu.PrefetchScalarGridSpec(
            num_scalar_prefetch=1,
            grid=grid,
            in_specs=in_specs,
            out_specs=out_specs,
            scratch_shapes=list(scratch),
        ),
        compiler_params=pltpu.CompilerParams(vmem_limit_bytes=(16 if name in SMALL else 60) << 20),
        cost_estimate=pl.CostEstimate(
            flops=int(MICROSECONDS[name] * COST_SCALE * 1e9), bytes_accessed=1, transcendentals=0
        ),
    )(scalars, *operands)


class Order:
    def __init__(self, scalars):
        self.scalars = scalars
        self.last = None

    def hold(self, *values):
        spec = pl.BlockSpec(memory_space=pl.ANY)
        held = pl.pallas_call(
            lambda *refs: None,
            name="hold",
            out_shape=[struct(v.shape, v.dtype) for v in values],
            in_specs=[spec] * (len(values) + 1),
            out_specs=[spec] * len(values),
            input_output_aliases={i: i for i in range(len(values))},
            cost_estimate=pl.CostEstimate(flops=1, bytes_accessed=1, transcendentals=0),
        )(*values, self.last)
        self.last = held[-1]
        return held

    def call(self, kernel, cfg, name, operands, in_specs, outs, out_specs, scratch=(), grid=(1,), scalars=None):
        kernel = functools.partial(kernel, cfg)
        scalars = self.scalars if scalars is None else scalars
        if self.last is not None:
            n = len(operands)
            operands = (*operands, self.last)
            in_specs = [*in_specs, pl.BlockSpec(memory_space=pl.ANY)]
            inner = kernel

            def kernel(scal, *refs):
                inner(scal, *refs[:n], *refs[n + 1 :])

        done = kernel_call(kernel, name, scalars, operands, in_specs, outs, out_specs, scratch, grid)
        self.last = done[-1] if isinstance(done, (list, tuple)) else done
        return done


def lanes_of(shape):
    return lax.broadcasted_iota(I32, shape, len(shape) - 1)


def columns_of(rows):
    n = rows[0].shape[1]
    filler = jnp.zeros((LANES - len(rows), n), F32)
    return jnp.concatenate(list(rows) + [filler], axis=0).T


def merged_stats(shares, splits, quarter):
    rows = []
    for step, share in enumerate(shares):
        value = share
        if quarter:
            value = jnp.concatenate(
                [value[:, (m ^ step) * quarter : ((m ^ step) + 1) * quarter] for m in range(splits)],
                axis=1,
            )
        rows.append((value[0:1], value[1:2]))
    top = rows[0][0]
    for peak, _ in rows[1:]:
        top = jnp.maximum(top, peak)
    total = rows[0][1] * jnp.exp(rows[0][0] - top)
    for peak, part in rows[1:]:
        total = total + part * jnp.exp(peak - top)
    return top, total


def target_columns(ids_ref):
    return columns_of([ids_ref[i : i + 1, :] for i in range(3)])


def send_kernel(cfg, scal, ids_ref, hid_ref, dt_ref, send_ref):
    groups, capacity = cfg
    tok = hid_ref.shape[0]
    width = max(LANES, 4 * groups)
    targets = target_columns(ids_ref)
    clus = targets[:, 1:2].astype(I32)
    word = targets[:, 2:3].astype(I32)
    member = (lanes_of((tok, width)) == clus).astype(F32).astype(BF16)
    row = lax.broadcasted_iota(I32, (tok, tok), 0)
    before = (lanes_of((tok, tok)) < row).astype(F32).astype(BF16)
    ranks = dot_nn(before, member)
    rank = jnp.sum(ranks * member.astype(F32), axis=1, keepdims=True).astype(I32)
    flat = lax.rem(clus, groups) * (4 * capacity) + lax.div(clus, groups) * capacity + rank
    flat = jnp.where(clus >= 0, flat, -1)
    place = (lanes_of((tok, tok)) == flat).astype(F32).astype(BF16)
    dt_ref[...] = place
    lane = lanes_of((tok, LANES))
    digits = jnp.where(
        lane == 0, lax.div(word, 256), jnp.where(lane == 1, lax.rem(word, 256), (lane == 2).astype(I32))
    )
    own = hid_ref.shape[1]
    send_ref[:, :own] = dot_tn(place, hid_ref[...]).astype(BF16)
    send_ref[:, own:] = dot_tn(place, digits.astype(F32).astype(BF16)).astype(BF16)


def logits_kernel(cfg, scal, *refs):
    n, clus_cols = cfg
    pieces, (w_ref, wc_ref, e_ref, ec_ref, st_ref, ex_ref) = refs[:n], refs[n : n + 6]
    peak_ref, sum_ref = refs[n + 6 :]
    j = pl.program_id(0)
    blocks = pl.num_programs(0)
    parts = []
    at = 0
    for piece in pieces:
        size = piece.shape[0]
        step = min(size, 256)
        parts += [(piece, i, at + i, step) for i in range(0, size, step)]
        at += size

    @pl.when(j == 0)
    def _():
        for piece, i, at, size in parts:
            out = slice(at, at + size)
            logits = dot_nn(piece[i : i + size, :], wc_ref[...])
            logits = jnp.where(lanes_of(logits.shape) < clus_cols, logits, -jnp.inf)
            peak = jnp.max(logits, axis=1, keepdims=True)
            expd = jnp.exp(logits - peak)
            ec_ref[out, :] = expd.astype(BF16)
            peak_ref[out, :] = peak
            sum_ref[out, :] = jnp.sum(expd, axis=1, keepdims=True)
            st_ref[out, :] = jnp.where(lanes_of((size, LANES)) == blocks, peak, 0.0)

    for piece, i, at, size in parts:
        out = slice(at, at + size)
        logits = dot_nn(piece[i : i + size, :], w_ref[...])
        before = peak_ref[out, :]
        peak = jnp.maximum(before, jnp.max(logits, axis=1, keepdims=True))
        expd = jnp.exp(logits - peak)
        e_ref[out, :] = expd.astype(BF16)
        total = sum_ref[out, :] * jnp.exp(before - peak) + jnp.sum(expd, axis=1, keepdims=True)
        peak_ref[out, :] = peak
        sum_ref[out, :] = total
        st_ref[out, :] = jnp.where(lanes_of((size, LANES)) == j, peak, st_ref[out, :])

    @pl.when(j == blocks - 1)
    def _():
        lane = lanes_of(st_ref.shape)
        both = jnp.where(lane == 0, peak_ref[...], jnp.where(lane == 1, sum_ref[...], 0.0))
        ex_ref[...] = both.T[:8]


def head_columns(cfg, shares, ids, permuted):
    splits, quarter = cfg
    top, total = merged_stats(shares, splits, quarter if permuted else 0)
    return columns_of([top, 1.0 / total, ids[0:1], ids[1:2]])


def head_block(expd, stats, lane, cols, target, first, limit):
    peak = jnp.sum(jnp.where(lanes_of(stats.shape) == lane, stats, 0.0), axis=1, keepdims=True)
    probs = expd.astype(F32) * (jnp.exp(peak - cols[:, 0:1]) * cols[:, 1:2])
    local = cols[:, target : target + 1].astype(I32) - first
    local = jnp.where(local < limit, local, -1)
    return jnp.where(lanes_of(probs.shape) == local, probs - 1.0, probs).astype(BF16)


def back_kernel(cfg, scal, e_ref, ec_ref, st_ref, ids_ref, *refs):
    splits, block, clus_cols = cfg
    shares, refs = refs[:splits], refs[splits:]
    w_ref, wc_ref, give_ref, keep_ref, g_ref, gc_ref, col_ref = refs
    i = pl.program_id(0)
    tok, word_cols = e_ref.shape
    blocks = word_cols // block

    @pl.when(i == 0)
    def _():
        col_ref[...] = head_columns((splits, 0), [share[...] for share in shares], ids_ref[...], False)
        for at in range(0, tok, LANES):
            rows = slice(at, at + LANES)
            cols, stats = col_ref[rows, :], st_ref[rows, :]
            for j in range(blocks):
                part = slice(j * block, (j + 1) * block)
                first = scal[0] * word_cols + j * block
                g_ref[rows, part] = head_block(e_ref[rows, part], stats, j, cols, 2, first, block)
            first = scal[0] * clus_cols
            gc_ref[rows, :] = head_block(ec_ref[rows, :], stats, blocks, cols, 3, first, clus_cols)

    out = dot_nt(g_ref[...], w_ref[...]) + dot_nt(gc_ref[...], wc_ref[...])

    @pl.when(i < splits // 2)
    def _():
        give_ref[0] = out.astype(BF16)

    @pl.when(i >= splits // 2)
    def _():
        keep_ref[0] = out.astype(BF16)


def turn_kernel(cfg, scal, *refs):
    near, n = cfg
    pieces, (out_ref,) = refs[:n], refs[n:]
    out_rows = out_ref.shape[0] // near
    at = 0
    for piece in pieces:
        size = piece.shape[0]
        turned = piece[...].T
        for i in range(near):
            to = pl.multiple_of((scal[2] ^ i) * out_rows, out_rows)
            out_ref[pl.ds(to, out_rows), at : at + size] = turned[i * out_rows : (i + 1) * out_rows]
        at += size


def weights_kernel(cfg, scal, t_ref, e0, e1, st0, st1, *refs):
    splits, quarter, clus_cols, word_cols, line, offset, last = cfg
    tok = e0.shape[0]
    block = e0.shape[1]
    i = pl.program_id(0)
    if last:
        col_ref, ec0, ec1, own_ref, near_ref, ownc_ref, nearc_ref, g_ref = refs
    else:
        ids0, ids1, *refs = refs
        shares0, shares1, refs = refs[:splits], refs[splits : 2 * splits], refs[2 * splits :]
        own_ref, near_ref, col_ref, g_ref = refs
    out_rows = own_ref.shape[0]

    def fill(first_ref, others_ref, lane, target, first, limit):
        for at in range(0, line * tok, LANES):
            source, stats, here = (first_ref, st0, at) if at < tok else (others_ref, st1, at - tok)
            rows = slice(here, here + LANES)
            g_ref[at : at + LANES, : source.shape[1]] = head_block(
                source[rows, :], stats[rows, :], lane, col_ref[at : at + LANES, :], target, first, limit
            )

    if not last:

        @pl.when(i == 0)
        def _():
            col_ref[:tok, :] = head_columns(
                (splits, quarter), [share[...] for share in shares0], ids0[...], False
            )
            for k in range(line - 1):
                part = slice(k * tok, (k + 1) * tok)
                col_ref[(k + 1) * tok : (k + 2) * tok, :] = head_columns(
                    (splits, quarter), [share[:, part] for share in shares1], ids1[:, part], True
                )

    j = i + offset
    fill(e0, e1, j, 2, scal[0] * word_cols + j * block, block)
    both = dot_nn(t_ref[...], g_ref[...]).astype(BF16)
    own_ref[...] = both[:out_rows]
    near_ref[...] = both[out_rows:]
    if last:

        @pl.when(i == pl.num_programs(0) - 1)
        def _():
            fill(ec0, ec1, word_cols // block, 3, scal[0] * clus_cols, clus_cols)
            both = dot_nn(t_ref[...], g_ref[:, :LANES]).astype(BF16)
            ownc_ref[...] = both[:out_rows]
            nearc_ref[...] = both[out_rows:]


def tail_logits_kernel(cfg, scal, *refs):
    splits = cfg
    pieces, refs = refs[:splits], refs[splits:]
    projections, outs, (red_ref, e_ref, ex_ref, acc_ref) = refs[:4], refs[4:8], refs[8:]
    i = pl.program_id(0)
    for m in range(splits):

        @pl.when(i == m)
        def _():
            at = 0
            for band, proj in enumerate(projections):
                part = slice(at, at + proj.shape[2])
                product = dot_nn(pieces[m][band], proj[0])
                acc_ref[:, part] = acc_ref[:, part] + product if m else product
                at += proj.shape[2]

    @pl.when(i == splits - 1)
    def _():
        tail_softmax(acc_ref, outs, red_ref, e_ref, ex_ref)


def tail_softmax(acc_ref, outs, red_ref, e_ref, ex_ref):
    red_ref[...] = acc_ref[...].astype(BF16)
    slots = red_ref.shape[0]
    at = to = 0
    ones = []
    for band, outw in enumerate(outs):
        size, cols = outw.shape[1:]
        logits = dot_nn(red_ref[:, at : at + size], outw[0])
        peak = jnp.max(logits, axis=1, keepdims=True)
        expd = jnp.exp(logits - peak)
        e_ref[:, to : to + cols] = expd.astype(BF16)
        ones += [peak, jnp.sum(expd, axis=1, keepdims=True)]
        at += size
        to += cols
    lane = lanes_of((slots, LANES))
    both = jnp.zeros((slots, LANES), F32)
    for i, one in enumerate(ones):
        both = jnp.where(lane == i, one, both)
    both = both.T
    for band in range(4):
        ex_ref[0:1, band * slots : (band + 1) * slots] = both[2 * band : 2 * band + 1]
        ex_ref[1:2, band * slots : (band + 1) * slots] = both[2 * band + 1 : 2 * band + 2]
    ex_ref[2:8, :] = jnp.zeros((6, ex_ref.shape[1]), F32)


def tail_grads_kernel(cfg, scal, red_ref, e_ref, digit_ref, *refs):
    splits = cfg
    shares, refs = refs[:splits], refs[splits:]
    outs, (go1, go2, go3, go4, out_ref) = refs[:4], refs[4:]
    slots = red_ref.shape[0]
    top, total = merged_stats([share[...] for share in shares], splits, 0)
    scale = jnp.exp(shares[0][0:1, :] - top) / total
    cols = columns_of([scale[:, b * slots : (b + 1) * slots] for b in range(4)])
    at = to = 0
    for band, (outw, go) in enumerate(zip(outs, (go1, go2, go3, go4))):
        size, vcols = outw.shape[1:]
        digits = digit_ref[band].astype(F32).astype(I32)
        word = digits[:, 0:1] * 256 + digits[:, 1:2]
        valid = digits[:, 2:3] > 0
        local = lax.rem(word, vcols * splits) - scal[0] * vcols
        probs = e_ref[:, to : to + vcols].astype(F32) * cols[:, band : band + 1]
        probs = jnp.where(lanes_of(probs.shape) == local, probs - 1.0, probs)
        dlog = jnp.where(valid, probs, 0.0).astype(BF16)
        out_ref[:, at : at + size] = dot_nt(dlog, outw[0])
        go[0] = dot_tn(red_ref[:, at : at + size], dlog).astype(BF16)
        at += size
        to += vcols


def tail_back_kernel(cfg, scal, part, far, rows_ref, p1, p2, p3, p4, g1, g2, g3, g4, back_ref):
    dred = (part[...].astype(F32) + far[...].astype(F32)).astype(BF16)
    at = 0
    for band, (proj, grad) in enumerate(zip((p1, p2, p3, p4), (g1, g2, g3, g4))):
        size = proj.shape[2]
        mine = dred[:, at : at + size]
        back_ref[band] = dot_nt(mine, proj[0]).astype(BF16)
        grad[0] = dot_tn(rows_ref[band], mine).astype(BF16)
        at += size


def add_kernel(cfg, scal, first_ref, second_ref, out_ref):
    total = first_ref[...].astype(F32) + second_ref[...].astype(F32)
    out_ref[...] = total.reshape(out_ref.shape).astype(BF16)


def final_kernel(cfg, scal, dt_ref, ret_ref, keep_ref, beside_ref, far_ref, out_ref):
    tail = dot_nn(dt_ref[...], ret_ref[...])
    head = keep_ref[0].astype(F32) + beside_ref[0].astype(F32) + far_ref[...].astype(F32)
    out_ref[...] = (head + tail).astype(BF16)


def body(
    hidden,
    target_cluster,
    target_word,
    head_words,
    head_clusters,
    proj_one,
    proj_two,
    proj_three,
    proj_four,
    out_one,
    out_two,
    out_three,
    out_four,
):
    groups = lax.axis_size("vocab")
    splits = lax.axis_size("tp")
    v_index = lax.axis_index("vocab")
    tp_index = lax.axis_index("tp")
    tok_rows, width = hidden.shape
    capacity = tok_rows // (4 * groups)
    clusters = 4 * groups
    slots = groups * capacity
    word_cols = head_words.shape[1]
    clus_cols = head_clusters.shape[1]
    own_width = width // splits
    line = 4
    near = groups // line
    line_index = v_index // near
    near_index = v_index % near
    quarter = tok_rows // splits
    out_rows = width // groups
    block = 512
    blocks = word_cols // block
    scalars = jnp.stack([tp_index, line_index, near_index]).astype(I32)
    order = Order(scalars)
    bits = [1 << i for i in range(splits.bit_length() - 1)]

    cluster_row = target_cluster.reshape(1, tok_rows)
    word_row = target_word.reshape(1, tok_rows)
    kind = lax.broadcasted_iota(I32, (8, tok_rows), 0)
    in_tail = cluster_row < clusters
    ids = jnp.where(
        kind == 0,
        jnp.where(in_tail, -1, word_row),
        jnp.where(kind == 1, jnp.where(in_tail, cluster_row, -1), word_row),
    ).astype(F32)
    moved_ids = [
        lax.ppermute(ids, "vocab", [(i, (i + step * near) % groups) for i in range(groups)])
        for step in range(1, line)
    ]

    def line_ids():
        moved = jnp.stack(moved_ids, axis=1)
        for bit in bits:
            parts = moved.reshape(8, line - 1, splits // (2 * bit), 2, bit * quarter)
            moved = jnp.where((tp_index // bit) % 2 == 1, parts[:, :, :, ::-1], parts)
        return moved.reshape(8, (line - 1) * tok_rows)

    ring = [(i, (i + near) % groups) for i in range(groups)]
    piece = lax.dynamic_slice_in_dim(hidden, tp_index * quarter, quarter, 0)
    from_line = {1: lax.ppermute(piece, "vocab", ring)}
    across = {}
    chunks = {0: [hidden]}

    def move_rows(stage):
        values = []
        if stage < line:
            values.append(from_line[stage])
        if stage > 1:
            values.append(across[stage - 1])
        values = order.hold(*values)
        if stage < line:
            held = values[0]
            if stage + 1 < line:
                from_line[stage + 1] = lax.ppermute(held, "vocab", ring)
            across[stage] = tp_swap(held, 2)
            chunks[stage] = [held, tp_swap(held, 1)]
        if stage > 1:
            chunks[stage - 1] += [values[-1], tp_swap(values[-1], 1)]

    clus_padded = jnp.pad(head_clusters, ((0, 0), (0, LANES - clus_cols)))
    row_block = pl.BlockSpec((tok_rows, block), lambda i, s: (0, i))
    lane_block = pl.BlockSpec((tok_rows, LANES), lambda i, s: (0, 0))
    stat_block = pl.BlockSpec((8, tok_rows), lambda i, s: (0, 0))

    def head_logits(pieces):
        tok = sum(p.shape[0] for p in pieces)
        return order.call(
            logits_kernel,
            (len(pieces), clus_cols),
            "head_logits" if len(pieces) == 1 else "line_logits",
            (*pieces, head_words, clus_padded),
            [whole(p) for p in pieces]
            + [pl.BlockSpec((width, block), lambda i, s: (0, i)), whole(clus_padded)],
            [
                struct((tok, word_cols), BF16),
                struct((tok, LANES), BF16),
                struct((tok, LANES), F32),
                struct((8, tok), F32),
            ],
            [
                pl.BlockSpec((tok, block), lambda i, s: (0, i)),
                pl.BlockSpec((tok, LANES), lambda i, s: (0, 0)),
                pl.BlockSpec((tok, LANES), lambda i, s: (0, 0)),
                pl.BlockSpec((8, tok), lambda i, s: (0, 0)),
            ],
            [pltpu.VMEM((tok, 1), F32)] * 2,
            (blocks,),
        )

    def shared(stats):
        return [tp_swap(stats, step) for step in range(1, splits)]

    def added(first, second, step, specs=None):
        out = struct(first.shape[-2:], BF16)
        total = order.call(
            add_kernel,
            None,
            "add",
            (first, second),
            specs or [whole(first), whole(second)],
            out,
            whole(out),
        )
        return total, tp_swap(total, step)

    projections = (proj_one, proj_two, proj_three, proj_four)
    outputs = (out_one, out_two, out_three, out_four)
    reduced_width = sum(p.shape[2] for p in projections)
    vocab_cols = sum(o.shape[2] for o in outputs)
    proj_specs = [
        pl.BlockSpec((1, own_width, p.shape[2]), lambda i, s: (0, s[0], 0)) for p in projections
    ]
    out_specs = [whole(o) for o in outputs]
    band_sums = struct((slots, reduced_width), F32)

    def tail_send():
        sent = struct((tok_rows, own_width + LANES), BF16)
        place = struct((tok_rows, tok_rows), BF16)
        dispatch, send = order.call(
            send_kernel,
            (groups, capacity),
            "send_rows",
            (ids, hidden),
            [whole(ids), pl.BlockSpec((tok_rows, own_width), lambda i, s: (0, s[0]))],
            [place, sent],
            [whole(place), whole(sent)],
        )
        recv = lax.all_to_all(
            send.reshape(groups, 4 * capacity, own_width + LANES),
            "vocab",
            split_axis=0,
            concat_axis=0,
            tiled=True,
        )
        rows = recv.reshape(groups, 4, capacity, own_width + LANES).transpose(1, 0, 2, 3)
        rows = rows.reshape(4, slots, own_width + LANES)
        return dispatch, rows[:, :, :own_width], rows[:, :, own_width:]

    def tail_logits():
        outs = [
            struct((slots, reduced_width), BF16),
            struct((slots, vocab_cols), BF16),
            struct((8, 4 * slots), F32),
        ]
        proj_parts = [
            pl.BlockSpec((1, own_width, p.shape[2]), lambda i, s: (0, s[0] ^ i, 0)) for p in projections
        ]
        return order.call(
            tail_logits_kernel,
            splits,
            "tail_logits",
            (*all_rows, *projections, *outputs),
            [whole(r) for r in all_rows] + proj_parts + out_specs,
            outs,
            [whole(o) for o in outs],
            [pltpu.VMEM((slots, reduced_width), F32)],
            (splits,),
        )

    def tail_grads():
        *grads_out, partial = order.call(
            tail_grads_kernel,
            splits,
            "tail_grads",
            (reduced, tail_expd, digits, tail_stats, *tail_shares, *outputs),
            [whole(reduced), whole(tail_expd), whole(digits)] + [whole(tail_stats)] * splits + out_specs,
            [struct(o.shape, BF16) for o in outputs] + [band_sums],
            out_specs + [whole(band_sums)],
        )
        return grads_out, partial, tp_swap(partial, 1)

    def tail_back():
        outs = [struct((1, own_width, p.shape[2]), BF16) for p in projections]
        outs.append(struct((4, slots, own_width), BF16))
        *grads_proj, back = order.call(
            tail_back_kernel,
            None,
            "tail_back",
            (part, far, rows, *projections),
            [whole(part), whole(far), whole(rows)] + proj_specs,
            outs,
            [whole(o) for o in outs],
        )
        back = back.reshape(4, groups, capacity, own_width).transpose(1, 0, 2, 3)
        returned = lax.all_to_all(
            back.reshape(groups, 4 * capacity, own_width),
            "vocab",
            split_axis=0,
            concat_axis=0,
            tiled=True,
        )
        return grads_proj, returned.reshape(tok_rows, own_width)

    def head_back():
        count = splits // 2

        def part_of(i):
            return jnp.where(i < count, 2 * i + 1, 2 * (i - count))

        pair = struct((count, tok_rows, own_width), BF16)
        give, keep = order.call(
            back_kernel,
            (splits, block, clus_cols),
            "head_back",
            (*own_expd, ids, own_stats, *early, head_words, clus_padded),
            [whole(v) for v in own_expd]
            + [stat_block] * (1 + splits)
            + [
                pl.BlockSpec((own_width, word_cols), lambda i, s: (s[0] ^ part_of(i), 0)),
                pl.BlockSpec((own_width, LANES), lambda i, s: (s[0] ^ part_of(i), 0)),
            ],
            [pair, pair],
            [
                pl.BlockSpec((1, tok_rows, own_width), lambda i, s: (jnp.minimum(i, count - 1), 0, 0)),
                pl.BlockSpec((1, tok_rows, own_width), lambda i, s: (jnp.maximum(i - count, 0), 0, 0)),
            ],
            [
                pltpu.VMEM((tok_rows, word_cols), BF16),
                pltpu.VMEM((tok_rows, LANES), BF16),
                pltpu.VMEM((tok_rows, LANES), F32),
            ],
            (splits,),
        )
        return keep, tp_swap(give, 1)

    def grad_hidden_step():
        out = struct((tok_rows, own_width), BF16)
        pair = pl.BlockSpec((1, tok_rows, own_width), lambda i, s: (0, 0, 0))
        return order.call(
            final_kernel,
            None,
            "grad_hidden",
            (dispatch, returned, back_keep, back_beside, back_far),
            [whole(dispatch), whole(returned), pair, pair, whole(back_far)],
            out,
            whole(out),
        )

    def turned_rows():
        pieces = [piece for step in range(line) for piece in chunks[step]]
        out = struct((near * out_rows, line * tok_rows), BF16)
        return order.call(
            turn_kernel,
            (near, len(pieces)),
            "turned_rows",
            pieces,
            [pl.BlockSpec((p.shape[0], near * out_rows), lambda i, s: (0, s[1])) for p in pieces],
            out,
            whole(out),
        )

    def weight_grads(half, count, columns):
        steps = blocks // count
        rest = (near - 1) * out_rows
        outs = [struct((out_rows, steps * block), BF16), struct((rest, steps * block), BF16)]
        specs = [pl.BlockSpec((o.shape[0], block), lambda i, s: (0, i)) for o in outs]
        operands = [turned, own_expd[0], line_expd[0], own_expd[2], line_expd[2]]
        in_specs = [
            whole(turned),
            pl.BlockSpec((tok_rows, block), lambda i, s: (0, i + half * steps)),
            pl.BlockSpec(((line - 1) * tok_rows, block), lambda i, s: (0, i + half * steps)),
            whole(own_expd[2]),
            whole(line_expd[2]),
        ]
        if columns is None:
            extra = [ids, line_ids(), own_stats, *early, *late]
            more = [struct((line * tok_rows, LANES), F32)]
        else:
            extra = [columns, own_expd[1], line_expd[1]]
            more = [struct((out_rows, LANES), BF16), struct((rest, LANES), BF16)]
        return order.call(
            weights_kernel,
            (splits, quarter, clus_cols, word_cols, line, half * steps, columns is not None),
            "head_weights",
            operands + extra,
            in_specs + [whole(v) for v in extra],
            outs + more,
            specs + [whole(o) for o in more],
            [pltpu.VMEM((line * tok_rows, block), BF16)],
            (steps,),
        )

    def near_sum(own, rest):
        total = own.astype(F32)
        for step in range(1, near):
            part = rest[(step - 1) * out_rows : step * out_rows]
            total = total + lax.ppermute(part, "vocab", xor_pairs(groups, step)).astype(F32)
        return total.astype(BF16)

    dispatch, rows, digits = tail_send()
    move_rows(1)
    *own_expd, own_stats = head_logits(chunks[0])
    early = shared(own_stats)
    move_rows(2)
    across_rows, beside_rows = tp_swap(rows, 2), tp_swap(rows, 1)
    back_keep, back_beside = head_back()
    (across_rows,) = order.hold(across_rows)
    all_rows = [rows, beside_rows, across_rows, tp_swap(across_rows, 1)]
    move_rows(3)
    reduced, tail_expd, tail_stats = tail_logits()
    tail_shares = shared(tail_stats)
    second = pl.BlockSpec((1, tok_rows, own_width), lambda i, s: (1, 0, 0))
    _, back_far = added(back_keep, back_beside, 2, [second, second])
    move_rows(4)
    turned = turned_rows()
    grads_out, part, beside = tail_grads()
    part, far = added(part, beside, 2)
    *line_expd, line_stats = head_logits([p for step in range(1, line) for p in chunks[step]])
    late = [line_stats] + shared(line_stats)
    grads_proj, returned = tail_back()
    own, rest, columns = weight_grads(0, 2, None)
    sums = [near_sum(own, rest)]
    own, rest, own_clus, rest_clus = weight_grads(1, 2, columns)
    sums.append(near_sum(own, rest))
    clus_sum = near_sum(own_clus, rest_clus)[:, :clus_cols]
    grad_hidden = grad_hidden_step()
    return (
        grad_hidden,
        jnp.concatenate(sums, axis=1),
        clus_sum,
        *grads_proj,
        *grads_out,
    )


def solution(mesh):
    return jax.shard_map(
        body,
        mesh=mesh,
        in_specs=(
            P("vocab", None),
            P("vocab", None),
            P("vocab"),
            P(None, "tp"),
            P(None, "tp"),
            P("vocab", None, None),
            P("vocab", None, None),
            P("vocab", None, None),
            P("vocab", None, None),
            P("vocab", None, "tp"),
            P("vocab", None, "tp"),
            P("vocab", None, "tp"),
            P("vocab", None, "tp"),
        ),
        out_specs=(
            P("vocab", "tp"),
            P("vocab", "tp"),
            P("vocab", "tp"),
            P("vocab", "tp", None),
            P("vocab", "tp", None),
            P("vocab", "tp", None),
            P("vocab", "tp", None),
            P("vocab", None, "tp"),
            P("vocab", None, "tp"),
            P("vocab", None, "tp"),
            P("vocab", None, "tp"),
        ),
        check_vma=False,
    )
```

```python
import functools

import jax
import jax.numpy as jnp
from jax import lax
from jax.experimental import pallas as pl
from jax.experimental.pallas import tpu as pltpu
from jax.sharding import PartitionSpec as P

F32 = jnp.float32
BF16 = jnp.bfloat16
I32 = jnp.int32
LANES = 128


def xor_pairs(size, step):
    return [(i, i ^ step) for i in range(size)]


def tp_swap(value, step):
    return lax.ppermute(value, "tp", xor_pairs(lax.axis_size("tp"), step))


def dot_nn(a, b):
    return lax.dot_general(a, b, (((1,), (0,)), ((), ())), preferred_element_type=F32)


def dot_nt(a, b):
    return lax.dot_general(a, b, (((1,), (1,)), ((), ())), preferred_element_type=F32)


def dot_tn(a, b):
    return lax.dot_general(a, b, (((0,), (0,)), ((), ())), preferred_element_type=F32)


def struct(shape, dtype):
    return jax.ShapeDtypeStruct(shape, dtype)


def whole(array):
    rank = len(array.shape)
    return pl.BlockSpec(array.shape, lambda *_: (0,) * rank)


COST_SCALE = 1.0
MICROSECONDS = {
    "send_rows": 3,
    "head_logits": 9,
    "line_logits": 20,
    "head_back": 9,
    "head_weights": 8,
    "tail_logits": 5,
    "tail_grads": 3,
    "tail_back": 3,
    "add": 1,
    "grad_hidden": 2,
}


SMALL = ("add",)


def kernel_call(kernel, name, scalars, operands, in_specs, outs, out_specs, scratch=(), grid=(1,)):
    return pl.pallas_call(
        kernel,
        name=name,
        out_shape=outs,
        grid_spec=pltpu.PrefetchScalarGridSpec(
            num_scalar_prefetch=1,
            grid=grid,
            in_specs=in_specs,
            out_specs=out_specs,
            scratch_shapes=list(scratch),
        ),
        compiler_params=pltpu.CompilerParams(vmem_limit_bytes=(16 if name in SMALL else 63) << 20),
        cost_estimate=pl.CostEstimate(
            flops=int(MICROSECONDS[name] * COST_SCALE * 1e9), bytes_accessed=1, transcendentals=0
        ),
    )(scalars, *operands)


class Order:
    def __init__(self, scalars):
        self.scalars = scalars
        self.last = None

    def hold(self, *values):
        spec = pl.BlockSpec(memory_space=pl.ANY)
        held = pl.pallas_call(
            lambda *refs: None,
            name="hold",
            out_shape=[struct(v.shape, v.dtype) for v in values],
            in_specs=[spec] * (len(values) + 1),
            out_specs=[spec] * len(values),
            input_output_aliases={i: i for i in range(len(values))},
            cost_estimate=pl.CostEstimate(flops=1, bytes_accessed=1, transcendentals=0),
        )(*values, self.last)
        self.last = held[-1]
        return held

    def call(self, kernel, cfg, name, operands, in_specs, outs, out_specs, scratch=(), grid=(1,), scalars=None):
        kernel = functools.partial(kernel, cfg)
        scalars = self.scalars if scalars is None else scalars
        if self.last is not None:
            n = len(operands)
            operands = (*operands, self.last)
            in_specs = [*in_specs, pl.BlockSpec(memory_space=pl.ANY)]
            inner = kernel

            def kernel(scal, *refs):
                inner(scal, *refs[:n], *refs[n + 1 :])

        done = kernel_call(kernel, name, scalars, operands, in_specs, outs, out_specs, scratch, grid)
        self.last = done[-1] if isinstance(done, (list, tuple)) else done
        return done


def lanes_of(shape):
    return lax.broadcasted_iota(I32, shape, len(shape) - 1)


def columns_of(rows):
    n = rows[0].shape[1]
    filler = jnp.zeros((LANES - len(rows), n), F32)
    return jnp.concatenate(list(rows) + [filler], axis=0).T


def merged_stats(shares, splits, quarter):
    rows = []
    for step, share in enumerate(shares):
        value = share
        if quarter:
            value = jnp.concatenate(
                [value[:, (m ^ step) * quarter : ((m ^ step) + 1) * quarter] for m in range(splits)],
                axis=1,
            )
        rows.append((value[0:1], value[1:2]))
    top = rows[0][0]
    for peak, _ in rows[1:]:
        top = jnp.maximum(top, peak)
    total = rows[0][1] * jnp.exp(rows[0][0] - top)
    for peak, part in rows[1:]:
        total = total + part * jnp.exp(peak - top)
    return top, total


def target_columns(ids_ref):
    return columns_of([ids_ref[i : i + 1, :] for i in range(3)])


def send_kernel(cfg, scal, ids_ref, hid_ref, dt_ref, send_ref):
    groups, capacity = cfg
    tok = hid_ref.shape[0]
    width = max(LANES, 4 * groups)
    targets = target_columns(ids_ref)
    clus = targets[:, 1:2].astype(I32)
    word = targets[:, 2:3].astype(I32)
    member = (lanes_of((tok, width)) == clus).astype(F32).astype(BF16)
    row = lax.broadcasted_iota(I32, (tok, tok), 0)
    before = (lanes_of((tok, tok)) < row).astype(F32).astype(BF16)
    ranks = dot_nn(before, member)
    rank = jnp.sum(ranks * member.astype(F32), axis=1, keepdims=True).astype(I32)
    flat = lax.rem(clus, groups) * (4 * capacity) + lax.div(clus, groups) * capacity + rank
    flat = jnp.where(clus >= 0, flat, -1)
    place = (lanes_of((tok, tok)) == flat).astype(F32).astype(BF16)
    dt_ref[...] = place
    lane = lanes_of((tok, LANES))
    digits = jnp.where(
        lane == 0, lax.div(word, 256), jnp.where(lane == 1, lax.rem(word, 256), (lane == 2).astype(I32))
    )
    own = hid_ref.shape[1]
    send_ref[:, :own] = dot_tn(place, hid_ref[...]).astype(BF16)
    send_ref[:, own:] = dot_tn(place, digits.astype(F32).astype(BF16)).astype(BF16)


def logits_kernel(cfg, scal, *refs):
    n, clus_cols, earlier = cfg
    pieces, refs = refs[:n], refs[n:]
    if earlier:
        earlier_ref, *refs = refs
    w_ref, wc_ref, e_ref, ec_ref, st_ref, turn_ref, ex_ref, peak_ref, sum_ref = refs
    j = pl.program_id(0)
    blocks = pl.num_programs(0)
    parts = []
    at = 0
    for piece in pieces:
        size = piece.shape[0]
        step = min(size, 256)
        parts += [(piece, i, at + i, step) for i in range(0, size, step)]
        at += size

    @pl.when(j == 0)
    def _():
        for piece, i, at, size in parts:
            out = slice(at, at + size)
            logits = dot_nn(piece[i : i + size, :], wc_ref[...])
            logits = jnp.where(lanes_of(logits.shape) < clus_cols, logits, -jnp.inf)
            peak = jnp.max(logits, axis=1, keepdims=True)
            expd = jnp.exp(logits - peak)
            ec_ref[out, :] = expd.astype(BF16)
            peak_ref[out, :] = peak
            sum_ref[out, :] = jnp.sum(expd, axis=1, keepdims=True)
            st_ref[out, :] = jnp.where(lanes_of((size, LANES)) == blocks, peak, 0.0)

    for piece, i, at, size in parts:
        out = slice(at, at + size)
        logits = dot_nn(piece[i : i + size, :], w_ref[...])
        before = peak_ref[out, :]
        peak = jnp.maximum(before, jnp.max(logits, axis=1, keepdims=True))
        expd = jnp.exp(logits - peak)
        e_ref[out, :] = expd.astype(BF16)
        total = sum_ref[out, :] * jnp.exp(before - peak) + jnp.sum(expd, axis=1, keepdims=True)
        peak_ref[out, :] = peak
        sum_ref[out, :] = total
        st_ref[out, :] = jnp.where(lanes_of((size, LANES)) == j, peak, st_ref[out, :])

    @pl.when(j == 1)
    def _():
        count = turn_ref.shape[0] * turn_ref.shape[1]
        first = pl.multiple_of(scal[1] * count, count)
        for piece, i, at, size in parts:
            turned_into(turn_ref, piece[i : i + size, pl.ds(first, count)], scal[2], at)

    @pl.when(j == blocks - 1)
    def _():
        lane = lanes_of(st_ref.shape)
        both = jnp.where(lane == 0, peak_ref[...], jnp.where(lane == 1, sum_ref[...], 0.0))
        if earlier:
            ex_ref[:, :earlier] = earlier_ref[...]
        ex_ref[:, earlier:] = both.T[:8]


WORD_LANE, CLUS_LANE = LANES - 2, LANES - 1


def head_columns(cfg, scal, shares, ids, stats, permuted):
    splits, quarter, word_cols, clus_cols = cfg
    top, total = merged_stats(shares, splits, quarter if permuted else 0)
    tp_index = scal[0]
    word = ids[0:1] - (tp_index * word_cols).astype(F32)
    clus = ids[1:2] - (tp_index * clus_cols).astype(F32)
    clus = jnp.where(clus < clus_cols, clus, -1.0)
    cols = columns_of([top, 1.0 / total, word, clus])
    scales = jnp.exp(stats - cols[:, 0:1]) * cols[:, 1:2]
    lane = lanes_of(scales.shape)
    return jnp.where(lane == WORD_LANE, cols[:, 2:3], jnp.where(lane == CLUS_LANE, cols[:, 3:4], scales))


def head_block(expd, cols, lane, target, first):
    scale = jnp.sum(jnp.where(lanes_of(cols.shape) == lane, cols, 0.0), axis=1, keepdims=True)
    local = cols[:, target : target + 1] - first
    probs = expd.astype(F32) * scale
    return jnp.where(lanes_of(probs.shape).astype(F32) == local, probs - 1.0, probs).astype(BF16)


def back_kernel(cfg, scal, e_ref, ec_ref, st_ref, ids_ref, *refs):
    splits, block, clus_cols = cfg
    shares, refs = refs[:splits], refs[splits:]
    w_ref, wc_ref, give_ref, keep_ref, g_ref, gc_ref, col_ref = refs
    i = pl.program_id(0)
    tok, word_cols = e_ref.shape
    blocks = word_cols // block

    @pl.when(i == 0)
    def _():
        cfg = (splits, 0, word_cols, clus_cols)
        col_ref[...] = head_columns(
            cfg, scal, [share[...] for share in shares], ids_ref[...], st_ref[...], False
        )
        for at in range(0, tok, LANES):
            rows = slice(at, at + LANES)
            cols = col_ref[rows, :]
            for j in range(blocks):
                part = slice(j * block, (j + 1) * block)
                g_ref[rows, part] = head_block(e_ref[rows, part], cols, j, WORD_LANE, float(j * block))
            gc_ref[rows, :] = head_block(ec_ref[rows, :], cols, blocks, CLUS_LANE, 0.0)

    out = dot_nt(g_ref[...], w_ref[...]) + dot_nt(gc_ref[...], wc_ref[...])

    @pl.when(i < splits // 2)
    def _():
        give_ref[0] = out.astype(BF16)

    @pl.when(i >= splits // 2)
    def _():
        keep_ref[0] = out.astype(BF16)


def turned_into(out_ref, value, near_index, at):
    turned = value.T
    near, out_rows, _ = out_ref.shape
    for i in range(near):
        out_ref[near_index ^ i, :, at : at + value.shape[0]] = turned[i * out_rows : (i + 1) * out_rows]


def weights_kernel(cfg, scal, *refs):
    splits, quarter, clus_cols, word_cols, sizes, offset, last = cfg
    n = len(sizes)
    turned, expds, refs = refs[:n], refs[n : 2 * n], refs[2 * n :]
    block = expds[0].shape[1]
    starts = [sum(sizes[:k]) for k in range(n)]
    i = pl.program_id(0)
    if last:
        col_ref, *clus, own_ref, near_ref, g_ref = refs
    else:
        stats, ids, refs = refs[:n], refs[n : 2 * n], refs[2 * n :]
        shares, refs = [refs[k * splits : (k + 1) * splits] for k in range(n)], refs[n * splits :]
        own_ref, near_ref, col_ref, g_ref = refs
    out_rows = own_ref.shape[0]

    def fill(sources, lane, target, first):
        for source, start, size in zip(sources, starts, sizes):
            for here in range(0, size, LANES):
                to = slice(start + here, start + here + LANES)
                g_ref[to, : source.shape[1]] = head_block(
                    source[here : here + LANES, :], col_ref[to, :], lane, target, first
                )

    def product(cols):
        total = None
        for ref, start, size in zip(turned, starts, sizes):
            rows = ref[...].reshape(ref.shape[0] * ref.shape[1], size)
            part = dot_nn(rows, g_ref[start : start + size, :cols])
            total = part if total is None else total + part
        return total.astype(BF16)

    if not last:

        @pl.when(i == 0)
        def _():
            cfg = (splits, quarter, word_cols, clus_cols)
            tok = sizes[0]
            for k in range(n):
                for here in range(0, sizes[k], tok):
                    part = slice(here, here + tok)
                    to = starts[k] + here
                    col_ref[to : to + tok, :] = head_columns(
                        cfg, scal, [share[:, part] for share in shares[k]], ids[k][:, part], stats[k][part, :], k > 0
                    )

    j = i + offset
    fill(expds, j, WORD_LANE, (j * block).astype(F32))
    both = product(block)
    here = pl.ds(pl.multiple_of(i * block, block), block)
    own_ref[:, here] = both[:out_rows]
    near_ref[:, here] = both[out_rows:]
    if last:

        @pl.when(i == pl.num_programs(0) - 1)
        def _():
            fill(clus, word_cols // block, CLUS_LANE, 0.0)
            both = product(LANES)
            own_ref[:, -LANES:] = both[:out_rows]
            near_ref[:, -LANES:] = both[out_rows:]


def tail_logits_kernel(cfg, scal, *refs):
    splits = cfg
    pieces, refs = refs[:splits], refs[splits:]
    projections, outs, (red_ref, e_ref, ex_ref, acc_ref) = refs[:4], refs[4:8], refs[8:]
    i = pl.program_id(0)
    for m in range(splits):

        @pl.when(i == m)
        def _():
            at = 0
            for band, proj in enumerate(projections):
                part = slice(at, at + proj.shape[2])
                product = dot_nn(pieces[m][band], proj[0])
                acc_ref[:, part] = acc_ref[:, part] + product if m else product
                at += proj.shape[2]

    @pl.when(i == splits - 1)
    def _():
        tail_softmax(acc_ref, outs, red_ref, e_ref, ex_ref)


def tail_softmax(acc_ref, outs, red_ref, e_ref, ex_ref):
    red_ref[...] = acc_ref[...].astype(BF16)
    slots = red_ref.shape[0]
    at = to = 0
    ones = []
    for band, outw in enumerate(outs):
        size, cols = outw.shape[1:]
        logits = dot_nn(red_ref[:, at : at + size], outw[0])
        peak = jnp.max(logits, axis=1, keepdims=True)
        expd = jnp.exp(logits - peak)
        e_ref[:, to : to + cols] = expd.astype(BF16)
        ones += [peak, jnp.sum(expd, axis=1, keepdims=True)]
        at += size
        to += cols
    lane = lanes_of((slots, LANES))
    both = jnp.zeros((slots, LANES), F32)
    for i, one in enumerate(ones):
        both = jnp.where(lane == i, one, both)
    both = both.T
    for band in range(4):
        ex_ref[0:1, band * slots : (band + 1) * slots] = both[2 * band : 2 * band + 1]
        ex_ref[1:2, band * slots : (band + 1) * slots] = both[2 * band + 1 : 2 * band + 2]
    ex_ref[2:8, :] = jnp.zeros((6, ex_ref.shape[1]), F32)


def tail_grads_kernel(cfg, scal, red_ref, e_ref, digit_ref, *refs):
    splits = cfg
    shares, refs = refs[:splits], refs[splits:]
    outs, (go1, go2, go3, go4, out_ref) = refs[:4], refs[4:]
    slots = red_ref.shape[0]
    top, total = merged_stats([share[...] for share in shares], splits, 0)
    scale = jnp.exp(shares[0][0:1, :] - top) / total
    cols = columns_of([scale[:, b * slots : (b + 1) * slots] for b in range(4)])
    at = to = 0
    for band, (outw, go) in enumerate(zip(outs, (go1, go2, go3, go4))):
        size, vcols = outw.shape[1:]
        digits = digit_ref[band].astype(F32).astype(I32)
        word = digits[:, 0:1] * 256 + digits[:, 1:2]
        valid = digits[:, 2:3] > 0
        local = lax.rem(word, vcols * splits) - scal[0] * vcols
        probs = e_ref[:, to : to + vcols].astype(F32) * cols[:, band : band + 1]
        probs = jnp.where(lanes_of(probs.shape) == local, probs - 1.0, probs)
        dlog = jnp.where(valid, probs, 0.0).astype(BF16)
        out_ref[:, at : at + size] = dot_nt(dlog, outw[0])
        go[0] = dot_tn(red_ref[:, at : at + size], dlog).astype(BF16)
        at += size
        to += vcols


def tail_back_kernel(cfg, scal, part, far, rows_ref, p1, p2, p3, p4, g1, g2, g3, g4, back_ref):
    dred = (part[...].astype(F32) + far[...].astype(F32)).astype(BF16)
    at = 0
    for band, (proj, grad) in enumerate(zip((p1, p2, p3, p4), (g1, g2, g3, g4))):
        size = proj.shape[2]
        mine = dred[:, at : at + size]
        back_ref[band] = dot_nt(mine, proj[0]).astype(BF16)
        grad[0] = dot_tn(rows_ref[band], mine).astype(BF16)
        at += size


def add_kernel(cfg, scal, first_ref, second_ref, out_ref):
    total = first_ref[...].astype(F32) + second_ref[...].astype(F32)
    out_ref[...] = total.reshape(out_ref.shape).astype(BF16)


def final_kernel(cfg, scal, dt_ref, ret_ref, keep_ref, beside_ref, far_ref, out_ref):
    tail = dot_nn(dt_ref[...], ret_ref[...])
    head = keep_ref[0].astype(F32) + beside_ref[0].astype(F32) + far_ref[...].astype(F32)
    out_ref[...] = (head + tail).astype(BF16)


def body(
    hidden,
    target_cluster,
    target_word,
    head_words,
    head_clusters,
    proj_one,
    proj_two,
    proj_three,
    proj_four,
    out_one,
    out_two,
    out_three,
    out_four,
):
    groups = lax.axis_size("vocab")
    splits = lax.axis_size("tp")
    v_index = lax.axis_index("vocab")
    tp_index = lax.axis_index("tp")
    tok_rows, width = hidden.shape
    capacity = tok_rows // (4 * groups)
    clusters = 4 * groups
    slots = groups * capacity
    word_cols = head_words.shape[1]
    clus_cols = head_clusters.shape[1]
    own_width = width // splits
    line = 4
    near = groups // line
    line_index = v_index // near
    near_index = v_index % near
    quarter = tok_rows // splits
    out_rows = width // groups
    block = 512
    blocks = word_cols // block
    scalars = jnp.stack([tp_index, line_index, near_index]).astype(I32)
    order = Order(scalars)
    bits = [1 << i for i in range(splits.bit_length() - 1)]

    cluster_row = target_cluster.reshape(1, tok_rows)
    word_row = target_word.reshape(1, tok_rows)
    kind = lax.broadcasted_iota(I32, (8, tok_rows), 0)
    in_tail = cluster_row < clusters
    ids = jnp.where(
        kind == 0,
        jnp.where(in_tail, -1, word_row),
        jnp.where(kind == 1, jnp.where(in_tail, cluster_row, -1), word_row),
    ).astype(F32)
    moved_ids = [
        lax.ppermute(ids, "vocab", [(i, (i + step * near) % groups) for i in range(groups)])
        for step in range(1, line)
    ]

    def line_ids():
        moved = jnp.stack(moved_ids, axis=1)
        for bit in bits:
            parts = moved.reshape(8, line - 1, splits // (2 * bit), 2, bit * quarter)
            moved = jnp.where((tp_index // bit) % 2 == 1, parts[:, :, :, ::-1], parts)
        return moved.reshape(8, (line - 1) * tok_rows)

    ring = [(i, (i + near) % groups) for i in range(groups)]
    piece = lax.dynamic_slice_in_dim(hidden, tp_index * quarter, quarter, 0)
    from_line = {1: lax.ppermute(piece, "vocab", ring)}
    across = {}
    chunks = {0: [hidden]}

    def move_rows(stage):
        values = []
        if stage < line:
            values.append(from_line[stage])
        if stage > 1:
            values.append(across[stage - 1])
        values = order.hold(*values)
        if stage < line:
            held = values[0]
            if stage + 1 < line:
                from_line[stage + 1] = lax.ppermute(held, "vocab", ring)
            across[stage] = tp_swap(held, 2)
            chunks[stage] = [held, tp_swap(held, 1)]
        if stage > 1:
            chunks[stage - 1] += [values[-1], tp_swap(values[-1], 1)]

    clus_padded = jnp.pad(head_clusters, ((0, 0), (0, LANES - clus_cols)))
    row_block = pl.BlockSpec((tok_rows, block), lambda i, s: (0, i))
    lane_block = pl.BlockSpec((tok_rows, LANES), lambda i, s: (0, 0))
    stat_block = pl.BlockSpec((8, tok_rows), lambda i, s: (0, 0))

    def head_logits(pieces, earlier):
        tok = sum(p.shape[0] for p in pieces)
        turned = struct((near, out_rows, tok), BF16)
        before = sum(e.shape[1] for e in earlier)
        stats = struct((8, before + tok), F32)
        return order.call(
            logits_kernel,
            (len(pieces), clus_cols, before),
            "head_logits" if len(pieces) == 1 else "line_logits",
            (*pieces, *earlier, head_words, clus_padded),
            [whole(p) for p in (*pieces, *earlier)]
            + [pl.BlockSpec((width, block), lambda i, s: (0, i)), whole(clus_padded)],
            [
                struct((tok, word_cols), BF16),
                struct((tok, LANES), BF16),
                struct((tok, LANES), F32),
                turned,
                stats,
            ],
            [
                pl.BlockSpec((tok, block), lambda i, s: (0, i)),
                pl.BlockSpec((tok, LANES), lambda i, s: (0, 0)),
                pl.BlockSpec((tok, LANES), lambda i, s: (0, 0)),
                whole(turned),
                whole(stats),
            ],
            [pltpu.VMEM((tok, 1), F32)] * 2,
            (blocks,),
        )

    def shared(stats):
        return [tp_swap(stats, step) for step in range(1, splits)]

    def added(first, second, specs=None):
        out = struct(first.shape[-2:], BF16)
        return order.call(
            add_kernel,
            None,
            "add",
            (first, second),
            specs or [whole(first), whole(second)],
            out,
            whole(out),
        )

    projections = (proj_one, proj_two, proj_three, proj_four)
    outputs = (out_one, out_two, out_three, out_four)
    reduced_width = sum(p.shape[2] for p in projections)
    vocab_cols = sum(o.shape[2] for o in outputs)
    proj_specs = [
        pl.BlockSpec((1, own_width, p.shape[2]), lambda i, s: (0, s[0], 0)) for p in projections
    ]
    out_specs = [whole(o) for o in outputs]
    band_sums = struct((slots, reduced_width), F32)

    def tail_rows():
        sent = struct((tok_rows, own_width + LANES), BF16)
        place = struct((tok_rows, tok_rows), BF16)
        return order.call(
            send_kernel,
            (groups, capacity),
            "send_rows",
            (ids, hidden),
            [whole(ids), pl.BlockSpec((tok_rows, own_width), lambda i, s: (0, s[0]))],
            [place, sent],
            [whole(place), whole(sent)],
        )
    def tail_send(send):
        recv = lax.all_to_all(
            send.reshape(groups, 4 * capacity, own_width + LANES),
            "vocab",
            split_axis=0,
            concat_axis=0,
            tiled=True,
        )
        rows = recv.reshape(groups, 4, capacity, own_width + LANES).transpose(1, 0, 2, 3)
        rows = rows.reshape(4, slots, own_width + LANES)
        return rows[:, :, :own_width], rows

    def tail_logits():
        outs = [
            struct((slots, reduced_width), BF16),
            struct((slots, vocab_cols), BF16),
            struct((8, 4 * slots), F32),
        ]
        proj_parts = [
            pl.BlockSpec((1, own_width, p.shape[2]), lambda i, s: (0, s[0] ^ i, 0)) for p in projections
        ]
        return order.call(
            tail_logits_kernel,
            splits,
            "tail_logits",
            (*all_rows, *projections, *outputs),
            [whole(r) for r in all_rows] + proj_parts + out_specs,
            outs,
            [whole(o) for o in outs],
            [pltpu.VMEM((slots, reduced_width), F32)],
            (splits,),
        )

    def tail_grads():
        *grads_out, partial = order.call(
            tail_grads_kernel,
            splits,
            "tail_grads",
            (reduced, tail_expd, digits, tail_stats, *tail_shares, *outputs),
            [
                whole(reduced),
                whole(tail_expd),
                pl.BlockSpec((4, slots, LANES), lambda i, s: (0, 0, own_width // LANES)),
            ]
            + [whole(tail_stats)] * splits + out_specs,
            [struct(o.shape, BF16) for o in outputs] + [band_sums],
            out_specs + [whole(band_sums)],
        )
        return grads_out, partial, tp_swap(partial, 1)

    def tail_back():
        outs = [struct((1, own_width, p.shape[2]), BF16) for p in projections]
        outs.append(struct((4, slots, own_width), BF16))
        *grads_proj, back = order.call(
            tail_back_kernel,
            None,
            "tail_back",
            (part, far, rows, *projections),
            [whole(part), whole(far), whole(rows)] + proj_specs,
            outs,
            [whole(o) for o in outs],
        )
        return grads_proj, back

    def tail_return(back):
        back = back.reshape(4, groups, capacity, own_width).transpose(1, 0, 2, 3)
        returned = lax.all_to_all(
            back.reshape(groups, 4 * capacity, own_width),
            "vocab",
            split_axis=0,
            concat_axis=0,
            tiled=True,
        )
        return returned.reshape(tok_rows, own_width)

    def head_back():
        count = splits // 2
        *own_expd, _ = head_groups[0]

        def part_of(i):
            return jnp.where(i < count, 2 * i + 1, 2 * (i - count))

        pair = struct((count, tok_rows, own_width), BF16)
        give, keep = order.call(
            back_kernel,
            (splits, block, clus_cols),
            "head_back",
            (*own_expd, ids, *early, head_words, clus_padded),
            [whole(v) for v in own_expd]
            + [stat_block] * (1 + splits)
            + [
                pl.BlockSpec((own_width, word_cols), lambda i, s: (s[0] ^ part_of(i), 0)),
                pl.BlockSpec((own_width, LANES), lambda i, s: (s[0] ^ part_of(i), 0)),
            ],
            [pair, pair],
            [
                pl.BlockSpec((1, tok_rows, own_width), lambda i, s: (jnp.minimum(i, count - 1), 0, 0)),
                pl.BlockSpec((1, tok_rows, own_width), lambda i, s: (jnp.maximum(i - count, 0), 0, 0)),
            ],
            [
                pltpu.VMEM((tok_rows, word_cols), BF16),
                pltpu.VMEM((tok_rows, LANES), BF16),
                pltpu.VMEM((tok_rows, LANES), F32),
            ],
            (splits,),
        )
        return keep, tp_swap(give, 1)

    def grad_hidden_step():
        out = struct((tok_rows, own_width), BF16)
        pair = pl.BlockSpec((1, tok_rows, own_width), lambda i, s: (0, 0, 0))
        return order.call(
            final_kernel,
            None,
            "grad_hidden",
            (dispatch, returned, back_keep, back_beside, back_far),
            [whole(dispatch), whole(returned), pair, pair, whole(back_far)],
            out,
            whole(out),
        )

    def weight_grads(first, steps, columns):
        rest = (near - 1) * out_rows
        sizes = tuple(group[0].shape[0] for group in head_groups)
        cols = steps * block + (LANES if columns is not None else 0)
        outs = [struct((out_rows, cols), BF16), struct((rest, cols), BF16)]
        expds, clus, stats, turned = zip(*head_groups)
        operands = [*turned, *expds]
        in_specs = [whole(t) for t in turned]
        in_specs += [pl.BlockSpec((size, block), lambda i, s: (0, i + first)) for size in sizes]
        if columns is None:
            others = line_ids()
            extra = [*stats, ids]
            in_specs += [whole(v) for v in extra]
            lanes = []
            at = 0
            for size in sizes[1:]:
                lanes.append(pl.BlockSpec((8, size), lambda i, s, place=at // size: (0, place)))
                at += size
            in_specs += lanes + [stat_block] * splits
            in_specs += [spec for spec in lanes for _ in range(splits)]
            extra += [others] * len(lanes) + early + late * len(lanes)
            outs.append(struct((line * tok_rows, LANES), F32))
        else:
            extra = [columns, *clus]
            in_specs += [whole(v) for v in extra]
        return order.call(
            weights_kernel,
            (splits, quarter, clus_cols, word_cols, sizes, first, columns is not None),
            "head_weights",
            operands + extra,
            in_specs,
            outs,
            [whole(o) for o in outs],
            [pltpu.VMEM((line * tok_rows, block), BF16)],
            (steps,),
        )

    def near_parts(own, rest):
        parts = [own]
        for step in range(1, near):
            part = rest[(step - 1) * out_rows : step * out_rows]
            parts.append(lax.ppermute(part, "vocab", xor_pairs(groups, step)))
        return parts

    def near_sum(parts):
        return sum(part.astype(F32) for part in parts).astype(BF16)

    head_groups = []

    def head_group(*steps, earlier=()):
        *group, mine = head_logits([p for step in steps for p in chunks[step]], earlier)
        head_groups.append(group)
        return mine

    dispatch, send = tail_rows()
    move_rows(1)
    early = head_group(0)
    early = [early] + shared(early)
    move_rows(2)
    rows, digits = tail_send(*order.hold(send))
    back_keep, back_beside = head_back()
    moved_ids = order.hold(*moved_ids)
    move_rows(3)
    late = head_group(1, 2)
    (rows,) = order.hold(rows)
    across_rows, beside_rows = tp_swap(rows, 2), tp_swap(rows, 1)
    move_rows(4)
    second = pl.BlockSpec((1, tok_rows, own_width), lambda i, s: (1, 0, 0))
    back_far = added(back_keep, back_beside, [second, second])
    late = head_group(3, earlier=(late,))
    late = [late] + shared(late)
    (across_rows,) = order.hold(across_rows)
    back_far = tp_swap(back_far, 2)
    all_rows = [rows, beside_rows, across_rows, tp_swap(across_rows, 1)]
    reduced, tail_expd, tail_stats = tail_logits()
    tail_shares = shared(tail_stats)
    (back_far,) = order.hold(back_far)
    grads_out, part, beside = tail_grads()
    part = added(part, beside)
    far = tp_swap(part, 2)
    ahead = blocks - 1
    *first_parts, columns = weight_grads(0, ahead, None)
    first_sum = near_parts(*first_parts)
    grads_proj, back = tail_back()
    returned = tail_return(back)
    second_sum = near_parts(*weight_grads(ahead, blocks - ahead, columns))
    grad_hidden = grad_hidden_step()
    second_sum = near_sum(order.hold(*second_sum))
    at = (blocks - ahead) * block
    sums = [near_sum(first_sum), second_sum[:, :at]]
    clus_sum = second_sum[:, at : at + clus_cols]
    return (
        grad_hidden,
        jnp.concatenate(sums, axis=1),
        clus_sum,
        *grads_proj,
        *grads_out,
    )


def solution(mesh):
    return jax.shard_map(
        body,
        mesh=mesh,
        in_specs=(
            P("vocab", None),
            P("vocab", None),
            P("vocab"),
            P(None, "tp"),
            P(None, "tp"),
            P("vocab", None, None),
            P("vocab", None, None),
            P("vocab", None, None),
            P("vocab", None, None),
            P("vocab", None, "tp"),
            P("vocab", None, "tp"),
            P("vocab", None, "tp"),
            P("vocab", None, "tp"),
        ),
        out_specs=(
            P("vocab", "tp"),
            P("vocab", "tp"),
            P("vocab", "tp"),
            P("vocab", "tp", None),
            P("vocab", "tp", None),
            P("vocab", "tp", None),
            P("vocab", "tp", None),
            P("vocab", None, "tp"),
            P("vocab", None, "tp"),
            P("vocab", None, "tp"),
            P("vocab", None, "tp"),
        ),
        check_vma=False,
    )
```

```python
import functools

import jax
import jax.numpy as jnp
from jax import lax
from jax.experimental import pallas as pl
from jax.experimental.pallas import tpu as pltpu
from jax.sharding import PartitionSpec as P

F32 = jnp.float32
BF16 = jnp.bfloat16
I32 = jnp.int32
LANES = 128


def xor_pairs(size, step):
    return [(i, i ^ step) for i in range(size)]


def tp_swap(value, step):
    return lax.ppermute(value, "tp", xor_pairs(lax.axis_size("tp"), step))


def dot_nn(a, b):
    return lax.dot_general(a, b, (((1,), (0,)), ((), ())), preferred_element_type=F32)


def dot_nt(a, b):
    return lax.dot_general(a, b, (((1,), (1,)), ((), ())), preferred_element_type=F32)


def dot_tn(a, b):
    return lax.dot_general(a, b, (((0,), (0,)), ((), ())), preferred_element_type=F32)


def struct(shape, dtype):
    return jax.ShapeDtypeStruct(shape, dtype)


def whole(array):
    rank = len(array.shape)
    return pl.BlockSpec(array.shape, lambda *_: (0,) * rank)


COST_SCALE = 1.0
MICROSECONDS = {
    "send_rows": 3,
    "head_logits": 9,
    "line_logits": 20,
    "head_back": 9,
    "head_weights": 8,
    "tail_logits": 5,
    "tail_grads": 3,
    "tail_back": 3,
    "add": 1,
    "grad_hidden": 2,
}


SMALL = ("add",)


def kernel_call(kernel, name, scalars, operands, in_specs, outs, out_specs, scratch=(), grid=(1,)):
    return pl.pallas_call(
        kernel,
        name=name,
        out_shape=outs,
        grid_spec=pltpu.PrefetchScalarGridSpec(
            num_scalar_prefetch=1,
            grid=grid,
            in_specs=in_specs,
            out_specs=out_specs,
            scratch_shapes=list(scratch),
        ),
        compiler_params=pltpu.CompilerParams(vmem_limit_bytes=(1023 * 64 if name not in SMALL else 16384) << 10),
        cost_estimate=pl.CostEstimate(
            flops=int(MICROSECONDS[name] * COST_SCALE * 1e9), bytes_accessed=1, transcendentals=0
        ),
    )(scalars, *operands)


class Order:
    def __init__(self, scalars):
        self.scalars = scalars
        self.last = None

    def hold(self, *values):
        spec = pl.BlockSpec(memory_space=pl.ANY)
        held = pl.pallas_call(
            lambda *refs: None,
            name="hold",
            out_shape=[struct(v.shape, v.dtype) for v in values],
            in_specs=[spec] * (len(values) + 1),
            out_specs=[spec] * len(values),
            input_output_aliases={i: i for i in range(len(values))},
            cost_estimate=pl.CostEstimate(flops=1, bytes_accessed=1, transcendentals=0),
        )(*values, self.last)
        self.last = held[-1]
        return held

    def call(self, kernel, cfg, name, operands, in_specs, outs, out_specs, scratch=(), grid=(1,), scalars=None):
        kernel = functools.partial(kernel, cfg)
        scalars = self.scalars if scalars is None else scalars
        if self.last is not None:
            n = len(operands)
            operands = (*operands, self.last)
            in_specs = [*in_specs, pl.BlockSpec(memory_space=pl.ANY)]
            inner = kernel

            def kernel(scal, *refs):
                inner(scal, *refs[:n], *refs[n + 1 :])

        done = kernel_call(kernel, name, scalars, operands, in_specs, outs, out_specs, scratch, grid)
        self.last = done[-1] if isinstance(done, (list, tuple)) else done
        return done


def lanes_of(shape):
    return lax.broadcasted_iota(I32, shape, len(shape) - 1)


def columns_of(rows):
    n = rows[0].shape[1]
    filler = jnp.zeros((LANES - len(rows), n), F32)
    return jnp.concatenate(list(rows) + [filler], axis=0).T


def merged_stats(shares, splits, quarter):
    rows = []
    for step, share in enumerate(shares):
        value = share
        if quarter:
            value = jnp.concatenate(
                [value[:, (m ^ step) * quarter : ((m ^ step) + 1) * quarter] for m in range(splits)],
                axis=1,
            )
        rows.append((value[0:1], value[1:2]))
    top = rows[0][0]
    for peak, _ in rows[1:]:
        top = jnp.maximum(top, peak)
    total = rows[0][1] * jnp.exp(rows[0][0] - top)
    for peak, part in rows[1:]:
        total = total + part * jnp.exp(peak - top)
    return top, total


def target_columns(ids_ref):
    return columns_of([ids_ref[i : i + 1, :] for i in range(3)])


def send_kernel(cfg, scal, ids_ref, hid_ref, dt_ref, send_ref):
    groups, capacity = cfg
    tok = hid_ref.shape[0]
    width = max(LANES, 4 * groups)
    targets = target_columns(ids_ref)
    clus = targets[:, 1:2].astype(I32)
    word = targets[:, 2:3].astype(I32)
    member = (lanes_of((tok, width)) == clus).astype(F32).astype(BF16)
    row = lax.broadcasted_iota(I32, (tok, tok), 0)
    before = (lanes_of((tok, tok)) < row).astype(F32).astype(BF16)
    ranks = dot_nn(before, member)
    rank = jnp.sum(ranks * member.astype(F32), axis=1, keepdims=True).astype(I32)
    flat = lax.rem(clus, groups) * (4 * capacity) + lax.div(clus, groups) * capacity + rank
    flat = jnp.where(clus >= 0, flat, -1)
    place = (lanes_of((tok, tok)) == flat).astype(F32).astype(BF16)
    dt_ref[...] = place
    lane = lanes_of((tok, LANES))
    digits = jnp.where(
        lane == 0, lax.div(word, 256), jnp.where(lane == 1, lax.rem(word, 256), (lane == 2).astype(I32))
    )
    own = hid_ref.shape[1]
    send_ref[:, :own] = dot_tn(place, hid_ref[...]).astype(BF16)
    send_ref[:, own:] = dot_tn(place, digits.astype(F32).astype(BF16)).astype(BF16)


def logits_kernel(cfg, scal, *refs):
    n, clus_cols, earlier = cfg
    pieces, refs = refs[:n], refs[n:]
    if earlier:
        earlier_ref, *refs = refs
    w_ref, wc_ref, e_ref, ec_ref, st_ref, turn_ref, ex_ref, peak_ref, sum_ref = refs
    j = pl.program_id(0)
    blocks = pl.num_programs(0)
    parts = []
    at = 0
    for piece in pieces:
        size = piece.shape[0]
        step = min(size, 256)
        parts += [(piece, i, at + i, step) for i in range(0, size, step)]
        at += size

    @pl.when(j == 0)
    def _():
        for piece, i, at, size in parts:
            out = slice(at, at + size)
            logits = dot_nn(piece[i : i + size, :], wc_ref[...])
            logits = jnp.where(lanes_of(logits.shape) < clus_cols, logits, -jnp.inf)
            peak = jnp.max(logits, axis=1, keepdims=True)
            expd = jnp.exp(logits - peak)
            ec_ref[out, :] = expd.astype(BF16)
            peak_ref[out, :] = peak
            sum_ref[out, :] = jnp.sum(expd, axis=1, keepdims=True)
            st_ref[out, :] = jnp.where(lanes_of((size, LANES)) == blocks, peak, 0.0)

    for piece, i, at, size in parts:
        out = slice(at, at + size)
        logits = dot_nn(piece[i : i + size, :], w_ref[...])
        before = peak_ref[out, :]
        peak = jnp.maximum(before, jnp.max(logits, axis=1, keepdims=True))
        expd = jnp.exp(logits - peak)
        e_ref[out, :] = expd.astype(BF16)
        total = sum_ref[out, :] * jnp.exp(before - peak) + jnp.sum(expd, axis=1, keepdims=True)
        peak_ref[out, :] = peak
        sum_ref[out, :] = total
        st_ref[out, :] = jnp.where(lanes_of((size, LANES)) == j, peak, st_ref[out, :])

    @pl.when(j == 1)
    def _():
        count = turn_ref.shape[0] * turn_ref.shape[1]
        first = pl.multiple_of(scal[1] * count, count)
        for piece, i, at, size in parts:
            turned_into(turn_ref, piece[i : i + size, pl.ds(first, count)], scal[2], at)

    @pl.when(j == blocks - 1)
    def _():
        lane = lanes_of(st_ref.shape)
        both = jnp.where(lane == 0, peak_ref[...], jnp.where(lane == 1, sum_ref[...], 0.0))
        if earlier:
            ex_ref[:, :earlier] = earlier_ref[...]
        ex_ref[:, earlier:] = both.T[:8]


WORD_LANE, CLUS_LANE = LANES - 2, LANES - 1


def head_columns(cfg, scal, shares, ids, stats, permuted):
    splits, quarter, word_cols, clus_cols = cfg
    top, total = merged_stats(shares, splits, quarter if permuted else 0)
    tp_index = scal[0]
    word = ids[0:1] - (tp_index * word_cols).astype(F32)
    clus = ids[1:2] - (tp_index * clus_cols).astype(F32)
    clus = jnp.where(clus < clus_cols, clus, -1.0)
    cols = columns_of([top, 1.0 / total, word, clus])
    scales = jnp.exp(stats - cols[:, 0:1]) * cols[:, 1:2]
    lane = lanes_of(scales.shape)
    return jnp.where(lane == WORD_LANE, cols[:, 2:3], jnp.where(lane == CLUS_LANE, cols[:, 3:4], scales))


def head_block(expd, cols, lane, target, first):
    scale = jnp.sum(jnp.where(lanes_of(cols.shape) == lane, cols, 0.0), axis=1, keepdims=True)
    local = cols[:, target : target + 1] - first
    probs = expd.astype(F32) * scale
    return jnp.where(lanes_of(probs.shape).astype(F32) == local, probs - 1.0, probs).astype(BF16)


def back_kernel(cfg, scal, e_ref, ec_ref, st_ref, ids_ref, *refs):
    splits, block, clus_cols = cfg
    shares, refs = refs[:splits], refs[splits:]
    w_ref, wc_ref, give_ref, keep_ref, g_ref, gc_ref, col_ref = refs
    i = pl.program_id(0)
    tok, word_cols = e_ref.shape
    blocks = word_cols // block

    @pl.when(i == 0)
    def _():
        cfg = (splits, 0, word_cols, clus_cols)
        col_ref[...] = head_columns(
            cfg, scal, [share[...] for share in shares], ids_ref[...], st_ref[...], False
        )
        for at in range(0, tok, LANES):
            rows = slice(at, at + LANES)
            cols = col_ref[rows, :]
            for j in range(blocks):
                part = slice(j * block, (j + 1) * block)
                g_ref[rows, part] = head_block(e_ref[rows, part], cols, j, WORD_LANE, float(j * block))
            gc_ref[rows, :] = head_block(ec_ref[rows, :], cols, blocks, CLUS_LANE, 0.0)

    out = dot_nt(g_ref[...], w_ref[...]) + dot_nt(gc_ref[...], wc_ref[...])

    @pl.when(i < splits // 2)
    def _():
        give_ref[0] = out.astype(BF16)

    @pl.when(i >= splits // 2)
    def _():
        keep_ref[0] = out.astype(BF16)


def turned_into(out_ref, value, near_index, at):
    turned = value.T
    near, out_rows, _ = out_ref.shape
    for i in range(near):
        out_ref[near_index ^ i, :, at : at + value.shape[0]] = turned[i * out_rows : (i + 1) * out_rows]


def weights_kernel(cfg, scal, *refs):
    splits, quarter, clus_cols, word_cols, sizes, offset, last = cfg
    n = len(sizes)
    turned, expds, refs = refs[:n], refs[n : 2 * n], refs[2 * n :]
    block = expds[0].shape[1]
    starts = [sum(sizes[:k]) for k in range(n)]
    i = pl.program_id(0)
    if last:
        col_ref, *clus, own_ref, near_ref, g_ref = refs
    else:
        stats, ids, refs = refs[:n], refs[n : 2 * n], refs[2 * n :]
        shares, refs = [refs[k * splits : (k + 1) * splits] for k in range(n)], refs[n * splits :]
        own_ref, near_ref, col_ref, g_ref = refs
    out_rows = own_ref.shape[0]

    def fill(sources, lane, target, first):
        for source, start, size in zip(sources, starts, sizes):
            for here in range(0, size, LANES):
                to = slice(start + here, start + here + LANES)
                g_ref[to, : source.shape[1]] = head_block(
                    source[here : here + LANES, :], col_ref[to, :], lane, target, first
                )

    def product(cols):
        total = None
        for ref, start, size in zip(turned, starts, sizes):
            rows = ref[...].reshape(ref.shape[0] * ref.shape[1], size)
            part = dot_nn(rows, g_ref[start : start + size, :cols])
            total = part if total is None else total + part
        return total.astype(BF16)

    if not last:

        @pl.when(i == 0)
        def _():
            cfg = (splits, quarter, word_cols, clus_cols)
            tok = sizes[0]
            for k in range(n):
                for here in range(0, sizes[k], tok):
                    part = slice(here, here + tok)
                    to = starts[k] + here
                    col_ref[to : to + tok, :] = head_columns(
                        cfg, scal, [share[:, part] for share in shares[k]], ids[k][:, part], stats[k][part, :], k > 0
                    )

    j = i + offset
    fill(expds, j, WORD_LANE, (j * block).astype(F32))
    both = product(block)
    here = pl.ds(pl.multiple_of(i * block, block), block)
    own_ref[:, here] = both[:out_rows]
    near_ref[:, here] = both[out_rows:]
    if last:

        @pl.when(i == pl.num_programs(0) - 1)
        def _():
            fill(clus, word_cols // block, CLUS_LANE, 0.0)
            both = product(LANES)
            own_ref[:, -LANES:] = both[:out_rows]
            near_ref[:, -LANES:] = both[out_rows:]


def tail_logits_kernel(cfg, scal, *refs):
    splits = cfg
    pieces, refs = refs[:splits], refs[splits:]
    projections, outs, (red_ref, e_ref, ex_ref, acc_ref) = refs[:4], refs[4:8], refs[8:]
    i = pl.program_id(0)
    for m in range(splits):

        @pl.when(i == m)
        def _():
            at = 0
            for band, proj in enumerate(projections):
                part = slice(at, at + proj.shape[2])
                product = dot_nn(pieces[m][band], proj[0])
                acc_ref[:, part] = acc_ref[:, part] + product if m else product
                at += proj.shape[2]

    @pl.when(i == splits - 1)
    def _():
        tail_softmax(acc_ref, outs, red_ref, e_ref, ex_ref)


def tail_softmax(acc_ref, outs, red_ref, e_ref, ex_ref):
    red_ref[...] = acc_ref[...].astype(BF16)
    slots = red_ref.shape[0]
    at = to = 0
    ones = []
    for band, outw in enumerate(outs):
        size, cols = outw.shape[1:]
        logits = dot_nn(red_ref[:, at : at + size], outw[0])
        peak = jnp.max(logits, axis=1, keepdims=True)
        expd = jnp.exp(logits - peak)
        e_ref[:, to : to + cols] = expd.astype(BF16)
        ones += [peak, jnp.sum(expd, axis=1, keepdims=True)]
        at += size
        to += cols
    lane = lanes_of((slots, LANES))
    both = jnp.zeros((slots, LANES), F32)
    for i, one in enumerate(ones):
        both = jnp.where(lane == i, one, both)
    both = both.T
    for band in range(4):
        ex_ref[0:1, band * slots : (band + 1) * slots] = both[2 * band : 2 * band + 1]
        ex_ref[1:2, band * slots : (band + 1) * slots] = both[2 * band + 1 : 2 * band + 2]
    ex_ref[2:8, :] = jnp.zeros((6, ex_ref.shape[1]), F32)


def tail_grads_kernel(cfg, scal, red_ref, e_ref, digit_ref, *refs):
    splits = cfg
    shares, refs = refs[:splits], refs[splits:]
    outs, (go1, go2, go3, go4, out_ref) = refs[:4], refs[4:]
    slots = red_ref.shape[0]
    top, total = merged_stats([share[...] for share in shares], splits, 0)
    scale = jnp.exp(shares[0][0:1, :] - top) / total
    cols = columns_of([scale[:, b * slots : (b + 1) * slots] for b in range(4)])
    at = to = 0
    for band, (outw, go) in enumerate(zip(outs, (go1, go2, go3, go4))):
        size, vcols = outw.shape[1:]
        digits = digit_ref[band].astype(F32).astype(I32)
        word = digits[:, 0:1] * 256 + digits[:, 1:2]
        valid = digits[:, 2:3] > 0
        local = lax.rem(word, vcols * splits) - scal[0] * vcols
        probs = e_ref[:, to : to + vcols].astype(F32) * cols[:, band : band + 1]
        probs = jnp.where(lanes_of(probs.shape) == local, probs - 1.0, probs)
        dlog = jnp.where(valid, probs, 0.0).astype(BF16)
        out_ref[:, at : at + size] = dot_nt(dlog, outw[0])
        go[0] = dot_tn(red_ref[:, at : at + size], dlog).astype(BF16)
        at += size
        to += vcols


def tail_back_kernel(in_place, scal, part, far, rows_ref, p1, p2, p3, p4, g1, g2, g3, g4, back_ref):
    own = p1.shape[1]
    dred = (part[...].astype(F32) + far[...].astype(F32)).astype(BF16)
    at = 0
    for band, (proj, grad) in enumerate(zip((p1, p2, p3, p4), (g1, g2, g3, g4))):
        size = proj.shape[2]
        mine = dred[:, at : at + size]
        back = dot_nt(mine, proj[0]).astype(BF16)
        if in_place:
            groups = back_ref.shape[0]
            rows = back.shape[0] // groups
            back_ref[:, band * rows : (band + 1) * rows, :] = back.reshape(groups, rows, own)
        else:
            back_ref[band] = back
        grad[0] = dot_tn(rows_ref[band], mine).astype(BF16)
        at += size


def add_kernel(cfg, scal, first_ref, second_ref, out_ref):
    total = first_ref[...].astype(F32) + second_ref[...].astype(F32)
    out_ref[...] = total.reshape(out_ref.shape).astype(BF16)


def final_kernel(cfg, scal, dt_ref, ret_ref, keep_ref, beside_ref, far_ref, out_ref):
    tail = dot_nn(dt_ref[...], ret_ref[...])
    head = keep_ref[0].astype(F32) + beside_ref[0].astype(F32) + far_ref[...].astype(F32)
    out_ref[...] = (head + tail).astype(BF16)


def body(
    hidden,
    target_cluster,
    target_word,
    head_words,
    head_clusters,
    proj_one,
    proj_two,
    proj_three,
    proj_four,
    out_one,
    out_two,
    out_three,
    out_four,
):
    groups = lax.axis_size("vocab")
    splits = lax.axis_size("tp")
    v_index = lax.axis_index("vocab")
    tp_index = lax.axis_index("tp")
    tok_rows, width = hidden.shape
    capacity = tok_rows // (4 * groups)
    clusters = 4 * groups
    slots = groups * capacity
    word_cols = head_words.shape[1]
    clus_cols = head_clusters.shape[1]
    own_width = width // splits
    line = 4
    near = groups // line
    line_index = v_index // near
    near_index = v_index % near
    quarter = tok_rows // splits
    out_rows = width // groups
    block = 512
    blocks = word_cols // block
    scalars = jnp.stack([tp_index, line_index, near_index]).astype(I32)
    order = Order(scalars)
    bits = [1 << i for i in range(splits.bit_length() - 1)]

    cluster_row = target_cluster.reshape(1, tok_rows)
    word_row = target_word.reshape(1, tok_rows)
    kind = lax.broadcasted_iota(I32, (8, tok_rows), 0)
    in_tail = cluster_row < clusters
    ids = jnp.where(
        kind == 0,
        jnp.where(in_tail, -1, word_row),
        jnp.where(kind == 1, jnp.where(in_tail, cluster_row, -1), word_row),
    ).astype(F32)
    moved_ids = [
        lax.ppermute(ids, "vocab", [(i, (i + step * near) % groups) for i in range(groups)])
        for step in range(1, line)
    ]

    def line_ids():
        moved = jnp.stack(moved_ids, axis=1)
        for bit in bits:
            parts = moved.reshape(8, line - 1, splits // (2 * bit), 2, bit * quarter)
            moved = jnp.where((tp_index // bit) % 2 == 1, parts[:, :, :, ::-1], parts)
        return moved.reshape(8, (line - 1) * tok_rows)

    ring = [(i, (i + near) % groups) for i in range(groups)]
    piece = lax.dynamic_slice_in_dim(hidden, tp_index * quarter, quarter, 0)
    from_line = {1: lax.ppermute(piece, "vocab", ring)}
    across = {}
    chunks = {0: [hidden]}

    def move_rows(stage):
        values = []
        if stage < line:
            values.append(from_line[stage])
        if stage > 1:
            values.append(across[stage - 1])
        values = order.hold(*values)
        if stage < line:
            held = values[0]
            if stage + 1 < line:
                from_line[stage + 1] = lax.ppermute(held, "vocab", ring)
            across[stage] = tp_swap(held, 2)
            chunks[stage] = [held, tp_swap(held, 1)]
        if stage > 1:
            chunks[stage - 1] += [values[-1], tp_swap(values[-1], 1)]

    clus_padded = jnp.pad(head_clusters, ((0, 0), (0, LANES - clus_cols)))
    row_block = pl.BlockSpec((tok_rows, block), lambda i, s: (0, i))
    lane_block = pl.BlockSpec((tok_rows, LANES), lambda i, s: (0, 0))
    stat_block = pl.BlockSpec((8, tok_rows), lambda i, s: (0, 0))

    def head_logits(pieces, earlier):
        tok = sum(p.shape[0] for p in pieces)
        turned = struct((near, out_rows, tok), BF16)
        before = sum(e.shape[1] for e in earlier)
        stats = struct((8, before + tok), F32)
        return order.call(
            logits_kernel,
            (len(pieces), clus_cols, before),
            "head_logits" if len(pieces) == 1 else "line_logits",
            (*pieces, *earlier, head_words, clus_padded),
            [whole(p) for p in (*pieces, *earlier)]
            + [pl.BlockSpec((width, block), lambda i, s: (0, i)), whole(clus_padded)],
            [
                struct((tok, word_cols), BF16),
                struct((tok, LANES), BF16),
                struct((tok, LANES), F32),
                turned,
                stats,
            ],
            [
                pl.BlockSpec((tok, block), lambda i, s: (0, i)),
                pl.BlockSpec((tok, LANES), lambda i, s: (0, 0)),
                pl.BlockSpec((tok, LANES), lambda i, s: (0, 0)),
                whole(turned),
                whole(stats),
            ],
            [pltpu.VMEM((tok, 1), F32)] * 2,
            (blocks,),
        )

    def shared(stats):
        return [tp_swap(stats, step) for step in range(1, splits)]

    def added(first, second, specs=None):
        out = struct(first.shape[-2:], BF16)
        return order.call(
            add_kernel,
            None,
            "add",
            (first, second),
            specs or [whole(first), whole(second)],
            out,
            whole(out),
        )

    projections = (proj_one, proj_two, proj_three, proj_four)
    outputs = (out_one, out_two, out_three, out_four)
    reduced_width = sum(p.shape[2] for p in projections)
    vocab_cols = sum(o.shape[2] for o in outputs)
    proj_specs = [
        pl.BlockSpec((1, own_width, p.shape[2]), lambda i, s: (0, s[0], 0)) for p in projections
    ]
    out_specs = [whole(o) for o in outputs]
    band_sums = struct((slots, reduced_width), F32)

    def tail_rows():
        sent = struct((tok_rows, own_width + LANES), BF16)
        place = struct((tok_rows, tok_rows), BF16)
        return order.call(
            send_kernel,
            (groups, capacity),
            "send_rows",
            (ids, hidden),
            [whole(ids), pl.BlockSpec((tok_rows, own_width), lambda i, s: (0, s[0]))],
            [place, sent],
            [whole(place), whole(sent)],
        )
    def tail_send(send):
        recv = lax.all_to_all(
            send.reshape(groups, 4 * capacity, own_width + LANES),
            "vocab",
            split_axis=0,
            concat_axis=0,
            tiled=True,
        )
        rows = recv.reshape(groups, 4, capacity, own_width + LANES).transpose(1, 0, 2, 3)
        rows = rows.reshape(4, slots, own_width + LANES)
        return rows[:, :, :own_width], rows

    def tail_logits():
        outs = [
            struct((slots, reduced_width), BF16),
            struct((slots, vocab_cols), BF16),
            struct((8, 4 * slots), F32),
        ]
        proj_parts = [
            pl.BlockSpec((1, own_width, p.shape[2]), lambda i, s: (0, s[0] ^ i, 0)) for p in projections
        ]
        return order.call(
            tail_logits_kernel,
            splits,
            "tail_logits",
            (*all_rows, *projections, *outputs),
            [whole(r) for r in all_rows] + proj_parts + out_specs,
            outs,
            [whole(o) for o in outs],
            [pltpu.VMEM((slots, reduced_width), F32)],
            (splits,),
        )

    def tail_grads():
        *grads_out, partial = order.call(
            tail_grads_kernel,
            splits,
            "tail_grads",
            (reduced, tail_expd, digits, tail_stats, *tail_shares, *outputs),
            [
                whole(reduced),
                whole(tail_expd),
                pl.BlockSpec((4, slots, LANES), lambda i, s: (0, 0, own_width // LANES)),
            ]
            + [whole(tail_stats)] * splits + out_specs,
            [struct(o.shape, BF16) for o in outputs] + [band_sums],
            out_specs + [whole(band_sums)],
        )
        return grads_out, partial, tp_swap(partial, 1)

    def tail_back():
        outs = [struct((1, own_width, p.shape[2]), BF16) for p in projections]
        in_place = capacity % 16 == 0
        outs.append(
            struct((groups, 4 * capacity, own_width) if in_place else (4, slots, own_width), BF16)
        )
        *grads_proj, back = order.call(
            tail_back_kernel,
            in_place,
            "tail_back",
            (part, far, rows, *projections),
            [whole(part), whole(far), whole(rows)] + proj_specs,
            outs,
            [whole(o) for o in outs],
        )
        return grads_proj, back

    def tail_return(back):
        if back.shape[0] != groups or capacity % 16:
            back = back.reshape(4, groups, capacity, own_width).transpose(1, 0, 2, 3)
        returned = lax.all_to_all(
            back.reshape(groups, 4 * capacity, own_width),
            "vocab",
            split_axis=0,
            concat_axis=0,
            tiled=True,
        )
        return returned.reshape(tok_rows, own_width)

    def head_back():
        count = splits // 2
        *own_expd, _ = head_groups[0]

        def part_of(i):
            return jnp.where(i < count, 2 * i + 1, 2 * (i - count))

        pair = struct((count, tok_rows, own_width), BF16)
        give, keep = order.call(
            back_kernel,
            (splits, block, clus_cols),
            "head_back",
            (*own_expd, ids, *early, head_words, clus_padded),
            [whole(v) for v in own_expd]
            + [stat_block] * (1 + splits)
            + [
                pl.BlockSpec((own_width, word_cols), lambda i, s: (s[0] ^ part_of(i), 0)),
                pl.BlockSpec((own_width, LANES), lambda i, s: (s[0] ^ part_of(i), 0)),
            ],
            [pair, pair],
            [
                pl.BlockSpec((1, tok_rows, own_width), lambda i, s: (jnp.minimum(i, count - 1), 0, 0)),
                pl.BlockSpec((1, tok_rows, own_width), lambda i, s: (jnp.maximum(i - count, 0), 0, 0)),
            ],
            [
                pltpu.VMEM((tok_rows, word_cols), BF16),
                pltpu.VMEM((tok_rows, LANES), BF16),
                pltpu.VMEM((tok_rows, LANES), F32),
            ],
            (splits,),
        )
        return keep, tp_swap(give, 1)

    def grad_hidden_step():
        out = struct((tok_rows, own_width), BF16)
        pair = pl.BlockSpec((1, tok_rows, own_width), lambda i, s: (0, 0, 0))
        return order.call(
            final_kernel,
            None,
            "grad_hidden",
            (dispatch, returned, back_keep, back_beside, back_far),
            [whole(dispatch), whole(returned), pair, pair, whole(back_far)],
            out,
            whole(out),
        )

    def weight_grads(first, steps, columns):
        rest = (near - 1) * out_rows
        sizes = tuple(group[0].shape[0] for group in head_groups)
        cols = steps * block + (LANES if columns is not None else 0)
        outs = [struct((out_rows, cols), BF16), struct((rest, cols), BF16)]
        expds, clus, stats, turned = zip(*head_groups)
        operands = [*turned, *expds]
        in_specs = [whole(t) for t in turned]
        in_specs += [pl.BlockSpec((size, block), lambda i, s: (0, i + first)) for size in sizes]
        if columns is None:
            others = line_ids()
            extra = [*stats, ids]
            in_specs += [whole(v) for v in extra]
            lanes = []
            at = 0
            for size in sizes[1:]:
                lanes.append(pl.BlockSpec((8, size), lambda i, s, place=at // size: (0, place)))
                at += size
            in_specs += lanes + [stat_block] * splits
            in_specs += [spec for spec in lanes for _ in range(splits)]
            extra += [others] * len(lanes) + early + late * len(lanes)
            outs.append(struct((line * tok_rows, LANES), F32))
        else:
            extra = [columns, *clus]
            in_specs += [whole(v) for v in extra]
        return order.call(
            weights_kernel,
            (splits, quarter, clus_cols, word_cols, sizes, first, columns is not None),
            "head_weights",
            operands + extra,
            in_specs,
            outs,
            [whole(o) for o in outs],
            [pltpu.VMEM((line * tok_rows, block), BF16)],
            (steps,),
        )

    def near_parts(own, rest):
        parts = [own]
        for step in range(1, near):
            part = rest[(step - 1) * out_rows : step * out_rows]
            parts.append(lax.ppermute(part, "vocab", xor_pairs(groups, step)))
        return parts

    def near_sum(parts):
        return sum(part.astype(F32) for part in parts).astype(BF16)

    head_groups = []

    def head_group(*steps, earlier=()):
        *group, mine = head_logits([p for step in steps for p in chunks[step]], earlier)
        head_groups.append(group)
        return mine

    dispatch, send = tail_rows()
    moved_ids = order.hold(*moved_ids)
    move_rows(1)
    early = head_group(0)
    early = [early] + shared(early)
    move_rows(2)
    rows, digits = tail_send(*order.hold(send))
    back_keep, back_beside = head_back()
    move_rows(3)
    late = head_group(1, 2)
    (rows,) = order.hold(rows)
    across_rows, beside_rows = tp_swap(rows, 2), tp_swap(rows, 1)
    move_rows(4)
    second = pl.BlockSpec((1, tok_rows, own_width), lambda i, s: (1, 0, 0))
    back_far = added(back_keep, back_beside, [second, second])
    late = head_group(3, earlier=(late,))
    late = [late] + shared(late)
    (across_rows,) = order.hold(across_rows)
    back_far = tp_swap(back_far, 2)
    all_rows = [rows, beside_rows, across_rows, tp_swap(across_rows, 1)]
    reduced, tail_expd, tail_stats = tail_logits()
    tail_shares = shared(tail_stats)
    (back_far,) = order.hold(back_far)
    grads_out, part, beside = tail_grads()
    part = added(part, beside)
    far = tp_swap(part, 2)
    ahead = blocks - 1
    *first_parts, columns = weight_grads(0, ahead, None)
    first_sum = near_parts(*first_parts)
    grads_proj, back = tail_back()
    returned = tail_return(back)
    second_sum = near_parts(*weight_grads(ahead, blocks - ahead, columns))
    grad_hidden = grad_hidden_step()
    second_sum = near_sum(order.hold(*second_sum))
    at = (blocks - ahead) * block
    sums = [near_sum(first_sum), second_sum[:, :at]]
    clus_sum = second_sum[:, at : at + clus_cols]
    return (
        grad_hidden,
        jnp.concatenate(sums, axis=1),
        clus_sum,
        *grads_proj,
        *grads_out,
    )


def solution(mesh):
    return jax.shard_map(
        body,
        mesh=mesh,
        in_specs=(
            P("vocab", None),
            P("vocab", None),
            P("vocab"),
            P(None, "tp"),
            P(None, "tp"),
            P("vocab", None, None),
            P("vocab", None, None),
            P("vocab", None, None),
            P("vocab", None, None),
            P("vocab", None, "tp"),
            P("vocab", None, "tp"),
            P("vocab", None, "tp"),
            P("vocab", None, "tp"),
        ),
        out_specs=(
            P("vocab", "tp"),
            P("vocab", "tp"),
            P("vocab", "tp"),
            P("vocab", "tp", None),
            P("vocab", "tp", None),
            P("vocab", "tp", None),
            P("vocab", "tp", None),
            P("vocab", None, "tp"),
            P("vocab", None, "tp"),
            P("vocab", None, "tp"),
            P("vocab", None, "tp"),
        ),
        check_vma=False,
    )
```

```python
import functools

import jax
import jax.numpy as jnp
from jax import lax
from jax.experimental import pallas as pl
from jax.experimental.pallas import tpu as pltpu
from jax.sharding import PartitionSpec as P

F32 = jnp.float32
BF16 = jnp.bfloat16
I32 = jnp.int32
LANES = 128


def xor_pairs(size, step):
    return [(i, i ^ step) for i in range(size)]


def tp_swap(value, step):
    return lax.ppermute(value, "tp", xor_pairs(lax.axis_size("tp"), step))


def dot_nn(a, b):
    return lax.dot_general(a, b, (((1,), (0,)), ((), ())), preferred_element_type=F32)


def dot_nt(a, b):
    return lax.dot_general(a, b, (((1,), (1,)), ((), ())), preferred_element_type=F32)


def dot_tn(a, b):
    return lax.dot_general(a, b, (((0,), (0,)), ((), ())), preferred_element_type=F32)


def struct(shape, dtype):
    return jax.ShapeDtypeStruct(shape, dtype)


def whole(array):
    rank = len(array.shape)
    return pl.BlockSpec(array.shape, lambda *_: (0,) * rank)


COST_SCALE = 1.0
MICROSECONDS = {
    "send_rows": 3,
    "head_logits": 9,
    "line_logits": 20,
    "head_back": 9,
    "head_weights": 8,
    "tail_logits": 5,
    "tail_grads": 3,
    "tail_back": 3,
    "add": 1,
    "grad_hidden": 2,
}


SMALL = ("add",)


def kernel_call(kernel, name, scalars, operands, in_specs, outs, out_specs, scratch=(), grid=(1,)):
    return pl.pallas_call(
        kernel,
        name=name,
        out_shape=outs,
        grid_spec=pltpu.PrefetchScalarGridSpec(
            num_scalar_prefetch=1,
            grid=grid,
            in_specs=in_specs,
            out_specs=out_specs,
            scratch_shapes=list(scratch),
        ),
        compiler_params=pltpu.CompilerParams(vmem_limit_bytes=(1023 * 64 if name not in SMALL else 16384) << 10),
        cost_estimate=pl.CostEstimate(
            flops=int(MICROSECONDS[name] * COST_SCALE * 1e9), bytes_accessed=1, transcendentals=0
        ),
    )(scalars, *operands)


class Order:
    def __init__(self, scalars):
        self.scalars = scalars
        self.last = None

    def hold(self, *values):
        spec = pl.BlockSpec(memory_space=pl.ANY)
        held = pl.pallas_call(
            lambda *refs: None,
            name="hold",
            out_shape=[struct(v.shape, v.dtype) for v in values],
            in_specs=[spec] * (len(values) + 1),
            out_specs=[spec] * len(values),
            input_output_aliases={i: i for i in range(len(values))},
            cost_estimate=pl.CostEstimate(flops=1, bytes_accessed=1, transcendentals=0),
        )(*values, self.last)
        self.last = held[-1]
        return held

    def call(self, kernel, cfg, name, operands, in_specs, outs, out_specs, scratch=(), grid=(1,), scalars=None):
        kernel = functools.partial(kernel, cfg)
        scalars = self.scalars if scalars is None else scalars
        if self.last is not None:
            n = len(operands)
            operands = (*operands, self.last)
            in_specs = [*in_specs, pl.BlockSpec(memory_space=pl.ANY)]
            inner = kernel

            def kernel(scal, *refs):
                inner(scal, *refs[:n], *refs[n + 1 :])

        done = kernel_call(kernel, name, scalars, operands, in_specs, outs, out_specs, scratch, grid)
        self.last = done[-1] if isinstance(done, (list, tuple)) else done
        return done


def lanes_of(shape):
    return lax.broadcasted_iota(I32, shape, len(shape) - 1)


def columns_of(rows):
    n = rows[0].shape[1]
    filler = jnp.zeros((LANES - len(rows), n), F32)
    return jnp.concatenate(list(rows) + [filler], axis=0).T


def merged_stats(shares, splits, quarter):
    rows = []
    for step, share in enumerate(shares):
        value = share
        if quarter:
            value = jnp.concatenate(
                [value[:, (m ^ step) * quarter : ((m ^ step) + 1) * quarter] for m in range(splits)],
                axis=1,
            )
        rows.append((value[0:1], value[1:2]))
    top = rows[0][0]
    for peak, _ in rows[1:]:
        top = jnp.maximum(top, peak)
    total = rows[0][1] * jnp.exp(rows[0][0] - top)
    for peak, part in rows[1:]:
        total = total + part * jnp.exp(peak - top)
    return top, total


def target_columns(ids_ref):
    return columns_of([ids_ref[i : i + 1, :] for i in range(3)])


def send_kernel(cfg, scal, ids_ref, hid_ref, dt_ref, send_ref):
    groups, capacity = cfg
    tok = hid_ref.shape[0]
    width = max(LANES, 4 * groups)
    targets = target_columns(ids_ref)
    clus = targets[:, 1:2].astype(I32)
    word = targets[:, 2:3].astype(I32)
    member = (lanes_of((tok, width)) == clus).astype(F32).astype(BF16)
    row = lax.broadcasted_iota(I32, (tok, tok), 0)
    before = (lanes_of((tok, tok)) < row).astype(F32).astype(BF16)
    ranks = dot_nn(before, member)
    rank = jnp.sum(ranks * member.astype(F32), axis=1, keepdims=True).astype(I32)
    flat = lax.rem(clus, groups) * (4 * capacity) + lax.div(clus, groups) * capacity + rank
    flat = jnp.where(clus >= 0, flat, -1)
    place = (lanes_of((tok, tok)) == flat).astype(F32).astype(BF16)
    dt_ref[...] = place
    lane = lanes_of((tok, LANES))
    digits = jnp.where(
        lane == 0, lax.div(word, 256), jnp.where(lane == 1, lax.rem(word, 256), (lane == 2).astype(I32))
    )
    own = hid_ref.shape[1]
    send_ref[:, :own] = dot_tn(place, hid_ref[...]).astype(BF16)
    send_ref[:, own:] = dot_tn(place, digits.astype(F32).astype(BF16)).astype(BF16)


def logits_kernel(cfg, scal, *refs):
    n, clus_cols, earlier = cfg
    pieces, refs = refs[:n], refs[n:]
    if earlier:
        earlier_ref, *refs = refs
    w_ref, wc_ref, e_ref, ec_ref, st_ref, turn_ref, ex_ref, peak_ref, sum_ref = refs
    j = pl.program_id(0)
    blocks = pl.num_programs(0)
    parts = []
    at = 0
    for piece in pieces:
        size = piece.shape[0]
        step = min(size, 256)
        parts += [(piece, i, at + i, step) for i in range(0, size, step)]
        at += size

    @pl.when(j == 0)
    def _():
        for piece, i, at, size in parts:
            out = slice(at, at + size)
            logits = dot_nn(piece[i : i + size, :], wc_ref[...])
            logits = jnp.where(lanes_of(logits.shape) < clus_cols, logits, -jnp.inf)
            peak = jnp.max(logits, axis=1, keepdims=True)
            expd = jnp.exp(logits - peak)
            ec_ref[out, :] = expd.astype(BF16)
            peak_ref[out, :] = peak
            sum_ref[out, :] = jnp.sum(expd, axis=1, keepdims=True)
            st_ref[out, :] = jnp.where(lanes_of((size, LANES)) == blocks, peak, 0.0)

    for piece, i, at, size in parts:
        out = slice(at, at + size)
        logits = dot_nn(piece[i : i + size, :], w_ref[...])
        before = peak_ref[out, :]
        peak = jnp.maximum(before, jnp.max(logits, axis=1, keepdims=True))
        expd = jnp.exp(logits - peak)
        e_ref[out, :] = expd.astype(BF16)
        total = sum_ref[out, :] * jnp.exp(before - peak) + jnp.sum(expd, axis=1, keepdims=True)
        peak_ref[out, :] = peak
        sum_ref[out, :] = total
        st_ref[out, :] = jnp.where(lanes_of((size, LANES)) == j, peak, st_ref[out, :])

    @pl.when(j == 1)
    def _():
        count = turn_ref.shape[0] * turn_ref.shape[1]
        first = pl.multiple_of(scal[1] * count, count)
        for piece, i, at, size in parts:
            turned_into(turn_ref, piece[i : i + size, pl.ds(first, count)], scal[2], at)

    @pl.when(j == blocks - 1)
    def _():
        lane = lanes_of(st_ref.shape)
        both = jnp.where(lane == 0, peak_ref[...], jnp.where(lane == 1, sum_ref[...], 0.0))
        if earlier:
            ex_ref[:, :earlier] = earlier_ref[...]
        ex_ref[:, earlier:] = both.T[:8]


WORD_LANE, CLUS_LANE = LANES - 2, LANES - 1


def head_columns(cfg, scal, shares, ids, stats, permuted):
    splits, quarter, word_cols, clus_cols = cfg
    top, total = merged_stats(shares, splits, quarter if permuted else 0)
    tp_index = scal[0]
    word = ids[0:1] - (tp_index * word_cols).astype(F32)
    clus = ids[1:2] - (tp_index * clus_cols).astype(F32)
    clus = jnp.where(clus < clus_cols, clus, -1.0)
    cols = columns_of([top, 1.0 / total, word, clus])
    scales = jnp.exp(stats - cols[:, 0:1]) * cols[:, 1:2]
    lane = lanes_of(scales.shape)
    return jnp.where(lane == WORD_LANE, cols[:, 2:3], jnp.where(lane == CLUS_LANE, cols[:, 3:4], scales))


def head_block(expd, cols, lane, target, first):
    scale = jnp.sum(jnp.where(lanes_of(cols.shape) == lane, cols, 0.0), axis=1, keepdims=True)
    local = cols[:, target : target + 1] - first
    probs = expd.astype(F32) * scale
    return jnp.where(lanes_of(probs.shape).astype(F32) == local, probs - 1.0, probs).astype(BF16)


def back_kernel(cfg, scal, e_ref, ec_ref, st_ref, ids_ref, *refs):
    splits, block, clus_cols = cfg
    shares, refs = refs[:splits], refs[splits:]
    w_ref, wc_ref, give_ref, keep_ref, g_ref, gc_ref, col_ref = refs
    i = pl.program_id(0)
    tok, word_cols = e_ref.shape
    blocks = word_cols // block

    @pl.when(i == 0)
    def _():
        cfg = (splits, 0, word_cols, clus_cols)
        col_ref[...] = head_columns(
            cfg, scal, [share[...] for share in shares], ids_ref[...], st_ref[...], False
        )
        for at in range(0, tok, LANES):
            rows = slice(at, at + LANES)
            cols = col_ref[rows, :]
            for j in range(blocks):
                part = slice(j * block, (j + 1) * block)
                g_ref[rows, part] = head_block(e_ref[rows, part], cols, j, WORD_LANE, float(j * block))
            gc_ref[rows, :] = head_block(ec_ref[rows, :], cols, blocks, CLUS_LANE, 0.0)

    out = dot_nt(g_ref[...], w_ref[...]) + dot_nt(gc_ref[...], wc_ref[...])

    @pl.when(i < splits // 2)
    def _():
        give_ref[0] = out.astype(BF16)

    @pl.when(i >= splits // 2)
    def _():
        keep_ref[0] = out.astype(BF16)


def turned_into(out_ref, value, near_index, at):
    turned = value.T
    near, out_rows, _ = out_ref.shape
    for i in range(near):
        out_ref[near_index ^ i, :, at : at + value.shape[0]] = turned[i * out_rows : (i + 1) * out_rows]


def weights_kernel(cfg, scal, *refs):
    splits, quarter, clus_cols, word_cols, sizes, offset, last = cfg
    n = len(sizes)
    turned, expds, refs = refs[:n], refs[n : 2 * n], refs[2 * n :]
    block = expds[0].shape[1]
    starts = [sum(sizes[:k]) for k in range(n)]
    i = pl.program_id(0)
    if last:
        col_ref, *clus, own_ref, near_ref, g_ref = refs
    else:
        stats, ids, refs = refs[:n], refs[n : 2 * n], refs[2 * n :]
        shares, refs = [refs[k * splits : (k + 1) * splits] for k in range(n)], refs[n * splits :]
        own_ref, near_ref, col_ref, g_ref = refs
    out_rows = own_ref.shape[0]

    def fill(sources, lane, target, first):
        for source, start, size in zip(sources, starts, sizes):
            for here in range(0, size, LANES):
                to = slice(start + here, start + here + LANES)
                g_ref[to, : source.shape[1]] = head_block(
                    source[here : here + LANES, :], col_ref[to, :], lane, target, first
                )

    def product(cols):
        total = None
        for ref, start, size in zip(turned, starts, sizes):
            rows = ref[...].reshape(ref.shape[0] * ref.shape[1], size)
            part = dot_nn(rows, g_ref[start : start + size, :cols])
            total = part if total is None else total + part
        return total.astype(BF16)

    if not last:

        @pl.when(i == 0)
        def _():
            cfg = (splits, quarter, word_cols, clus_cols)
            tok = sizes[0]
            for k in range(n):
                for here in range(0, sizes[k], tok):
                    part = slice(here, here + tok)
                    to = starts[k] + here
                    col_ref[to : to + tok, :] = head_columns(
                        cfg, scal, [share[:, part] for share in shares[k]], ids[k][:, part], stats[k][part, :], k > 0
                    )

    j = i + offset
    fill(expds, j, WORD_LANE, (j * block).astype(F32))
    both = product(block)
    here = pl.ds(pl.multiple_of(i * block, block), block)
    own_ref[:, here] = both[:out_rows]
    near_ref[:, here] = both[out_rows:]
    if last:

        @pl.when(i == pl.num_programs(0) - 1)
        def _():
            fill(clus, word_cols // block, CLUS_LANE, 0.0)
            both = product(LANES)
            own_ref[:, -LANES:] = both[:out_rows]
            near_ref[:, -LANES:] = both[out_rows:]


def tail_logits_kernel(cfg, scal, *refs):
    splits = cfg
    pieces, refs = refs[:splits], refs[splits:]
    projections, outs, (red_ref, e_ref, ex_ref, acc_ref) = refs[:4], refs[4:8], refs[8:]
    i = pl.program_id(0)
    for m in range(splits):

        @pl.when(i == m)
        def _():
            at = 0
            for band, proj in enumerate(projections):
                part = slice(at, at + proj.shape[2])
                product = dot_nn(pieces[m][band], proj[0])
                acc_ref[:, part] = acc_ref[:, part] + product if m else product
                at += proj.shape[2]

    @pl.when(i == splits - 1)
    def _():
        tail_softmax(acc_ref, outs, red_ref, e_ref, ex_ref)


def tail_softmax(acc_ref, outs, red_ref, e_ref, ex_ref):
    red_ref[...] = acc_ref[...].astype(BF16)
    slots = red_ref.shape[0]
    at = to = 0
    ones = []
    for band, outw in enumerate(outs):
        size, cols = outw.shape[1:]
        logits = dot_nn(red_ref[:, at : at + size], outw[0])
        peak = jnp.max(logits, axis=1, keepdims=True)
        expd = jnp.exp(logits - peak)
        e_ref[:, to : to + cols] = expd.astype(BF16)
        ones += [peak, jnp.sum(expd, axis=1, keepdims=True)]
        at += size
        to += cols
    lane = lanes_of((slots, LANES))
    both = jnp.zeros((slots, LANES), F32)
    for i, one in enumerate(ones):
        both = jnp.where(lane == i, one, both)
    both = both.T
    for band in range(4):
        ex_ref[0:1, band * slots : (band + 1) * slots] = both[2 * band : 2 * band + 1]
        ex_ref[1:2, band * slots : (band + 1) * slots] = both[2 * band + 1 : 2 * band + 2]
    ex_ref[2:8, :] = jnp.zeros((6, ex_ref.shape[1]), F32)


def tail_grads_kernel(cfg, scal, red_ref, e_ref, digit_ref, *refs):
    splits = cfg
    shares, refs = refs[:splits], refs[splits:]
    outs, (go1, go2, go3, go4, out_ref) = refs[:4], refs[4:]
    slots = red_ref.shape[0]
    top, total = merged_stats([share[...] for share in shares], splits, 0)
    scale = jnp.exp(shares[0][0:1, :] - top) / total
    cols = columns_of([scale[:, b * slots : (b + 1) * slots] for b in range(4)])
    at = to = 0
    for band, (outw, go) in enumerate(zip(outs, (go1, go2, go3, go4))):
        size, vcols = outw.shape[1:]
        digits = digit_ref[band].astype(F32).astype(I32)
        word = digits[:, 0:1] * 256 + digits[:, 1:2]
        valid = digits[:, 2:3] > 0
        local = lax.rem(word, vcols * splits) - scal[0] * vcols
        probs = e_ref[:, to : to + vcols].astype(F32) * cols[:, band : band + 1]
        probs = jnp.where(lanes_of(probs.shape) == local, probs - 1.0, probs)
        dlog = jnp.where(valid, probs, 0.0).astype(BF16)
        out_ref[:, at : at + size] = dot_nt(dlog, outw[0])
        go[0] = dot_tn(red_ref[:, at : at + size], dlog).astype(BF16)
        at += size
        to += vcols


def tail_back_kernel(in_place, scal, part, far, rows_ref, p1, p2, p3, p4, g1, g2, g3, g4, back_ref):
    own = p1.shape[1]
    dred = (part[...].astype(F32) + far[...].astype(F32)).astype(BF16)
    at = 0
    for band, (proj, grad) in enumerate(zip((p1, p2, p3, p4), (g1, g2, g3, g4))):
        size = proj.shape[2]
        mine = dred[:, at : at + size]
        back = dot_nt(mine, proj[0]).astype(BF16)
        if in_place:
            groups = back_ref.shape[0]
            rows = back.shape[0] // groups
            back_ref[:, band * rows : (band + 1) * rows, :] = back.reshape(groups, rows, own)
        else:
            back_ref[band] = back
        grad[0] = dot_tn(rows_ref[band], mine).astype(BF16)
        at += size


def add_kernel(cfg, scal, first_ref, second_ref, out_ref):
    total = first_ref[...].astype(F32) + second_ref[...].astype(F32)
    out_ref[...] = total.reshape(out_ref.shape).astype(BF16)


def final_kernel(cfg, scal, dt_ref, ret_ref, keep_ref, beside_ref, far_ref, out_ref):
    tail = dot_nn(dt_ref[...], ret_ref[...])
    head = keep_ref[0].astype(F32) + beside_ref[0].astype(F32) + far_ref[...].astype(F32)
    out_ref[...] = (head + tail).astype(BF16)


def body(
    hidden,
    target_cluster,
    target_word,
    head_words,
    head_clusters,
    proj_one,
    proj_two,
    proj_three,
    proj_four,
    out_one,
    out_two,
    out_three,
    out_four,
):
    groups = lax.axis_size("vocab")
    splits = lax.axis_size("tp")
    v_index = lax.axis_index("vocab")
    tp_index = lax.axis_index("tp")
    tok_rows, width = hidden.shape
    capacity = tok_rows // (4 * groups)
    clusters = 4 * groups
    slots = groups * capacity
    word_cols = head_words.shape[1]
    clus_cols = head_clusters.shape[1]
    own_width = width // splits
    line = 4
    near = groups // line
    line_index = v_index // near
    near_index = v_index % near
    quarter = tok_rows // splits
    out_rows = width // groups
    block = 512
    blocks = word_cols // block
    scalars = jnp.stack([tp_index, line_index, near_index]).astype(I32)
    order = Order(scalars)
    bits = [1 << i for i in range(splits.bit_length() - 1)]

    cluster_row = target_cluster.reshape(1, tok_rows)
    word_row = target_word.reshape(1, tok_rows)
    kind = lax.broadcasted_iota(I32, (8, tok_rows), 0)
    in_tail = cluster_row < clusters
    ids = jnp.where(
        kind == 0,
        jnp.where(in_tail, -1, word_row),
        jnp.where(kind == 1, jnp.where(in_tail, cluster_row, -1), word_row),
    ).astype(F32)
    moved_ids = [
        lax.ppermute(ids, "vocab", [(i, (i + step * near) % groups) for i in range(groups)])
        for step in range(1, line)
    ]

    def line_ids():
        moved = jnp.stack(moved_ids, axis=1)
        for bit in bits:
            parts = moved.reshape(8, line - 1, splits // (2 * bit), 2, bit * quarter)
            moved = jnp.where((tp_index // bit) % 2 == 1, parts[:, :, :, ::-1], parts)
        return moved.reshape(8, (line - 1) * tok_rows)

    ring = [(i, (i + near) % groups) for i in range(groups)]
    piece = lax.dynamic_slice_in_dim(hidden, tp_index * quarter, quarter, 0)
    from_line = {1: lax.ppermute(piece, "vocab", ring)}
    across = {}
    chunks = {0: [hidden]}

    def move_rows(stage):
        values = []
        if stage < line:
            values.append(from_line[stage])
        if stage > 1:
            values.append(across[stage - 1])
        values = order.hold(*values)
        if stage < line:
            held = values[0]
            if stage + 1 < line:
                from_line[stage + 1] = lax.ppermute(held, "vocab", ring)
            across[stage] = tp_swap(held, 2)
            chunks[stage] = [held, tp_swap(held, 1)]
        if stage > 1:
            chunks[stage - 1] += [values[-1], tp_swap(values[-1], 1)]

    clus_padded = jnp.pad(head_clusters, ((0, 0), (0, LANES - clus_cols)))
    row_block = pl.BlockSpec((tok_rows, block), lambda i, s: (0, i))
    lane_block = pl.BlockSpec((tok_rows, LANES), lambda i, s: (0, 0))
    stat_block = pl.BlockSpec((8, tok_rows), lambda i, s: (0, 0))

    def head_logits(pieces, earlier):
        tok = sum(p.shape[0] for p in pieces)
        turned = struct((near, out_rows, tok), BF16)
        before = sum(e.shape[1] for e in earlier)
        stats = struct((8, before + tok), F32)
        return order.call(
            logits_kernel,
            (len(pieces), clus_cols, before),
            "head_logits" if len(pieces) == 1 else "line_logits",
            (*pieces, *earlier, head_words, clus_padded),
            [whole(p) for p in (*pieces, *earlier)]
            + [pl.BlockSpec((width, block), lambda i, s: (0, i)), whole(clus_padded)],
            [
                struct((tok, word_cols), BF16),
                struct((tok, LANES), BF16),
                struct((tok, LANES), F32),
                turned,
                stats,
            ],
            [
                pl.BlockSpec((tok, block), lambda i, s: (0, i)),
                pl.BlockSpec((tok, LANES), lambda i, s: (0, 0)),
                pl.BlockSpec((tok, LANES), lambda i, s: (0, 0)),
                whole(turned),
                whole(stats),
            ],
            [pltpu.VMEM((tok, 1), F32)] * 2,
            (blocks,),
        )

    def shared(stats):
        return [tp_swap(stats, step) for step in range(1, splits)]

    def added(first, second, specs=None):
        out = struct(first.shape[-2:], BF16)
        return order.call(
            add_kernel,
            None,
            "add",
            (first, second),
            specs or [whole(first), whole(second)],
            out,
            whole(out),
        )

    projections = (proj_one, proj_two, proj_three, proj_four)
    outputs = (out_one, out_two, out_three, out_four)
    reduced_width = sum(p.shape[2] for p in projections)
    vocab_cols = sum(o.shape[2] for o in outputs)
    proj_specs = [
        pl.BlockSpec((1, own_width, p.shape[2]), lambda i, s: (0, s[0], 0)) for p in projections
    ]
    out_specs = [whole(o) for o in outputs]
    band_sums = struct((slots, reduced_width), F32)

    def tail_rows():
        sent = struct((tok_rows, own_width + LANES), BF16)
        place = struct((tok_rows, tok_rows), BF16)
        return order.call(
            send_kernel,
            (groups, capacity),
            "send_rows",
            (ids, hidden),
            [whole(ids), pl.BlockSpec((tok_rows, own_width), lambda i, s: (0, s[0]))],
            [place, sent],
            [whole(place), whole(sent)],
        )
    def tail_send(send):
        recv = lax.all_to_all(
            send.reshape(groups, 4 * capacity, own_width + LANES),
            "vocab",
            split_axis=0,
            concat_axis=0,
            tiled=True,
        )
        rows = recv.reshape(groups, 4, capacity, own_width + LANES).transpose(1, 0, 2, 3)
        rows = rows.reshape(4, slots, own_width + LANES)
        return rows[:, :, :own_width], rows

    def tail_logits():
        outs = [
            struct((slots, reduced_width), BF16),
            struct((slots, vocab_cols), BF16),
            struct((8, 4 * slots), F32),
        ]
        proj_parts = [
            pl.BlockSpec((1, own_width, p.shape[2]), lambda i, s: (0, s[0] ^ i, 0)) for p in projections
        ]
        return order.call(
            tail_logits_kernel,
            splits,
            "tail_logits",
            (*all_rows, *projections, *outputs),
            [whole(r) for r in all_rows] + proj_parts + out_specs,
            outs,
            [whole(o) for o in outs],
            [pltpu.VMEM((slots, reduced_width), F32)],
            (splits,),
        )

    def tail_grads():
        *grads_out, partial = order.call(
            tail_grads_kernel,
            splits,
            "tail_grads",
            (reduced, tail_expd, digits, tail_stats, *tail_shares, *outputs),
            [
                whole(reduced),
                whole(tail_expd),
                pl.BlockSpec((4, slots, LANES), lambda i, s: (0, 0, own_width // LANES)),
            ]
            + [whole(tail_stats)] * splits + out_specs,
            [struct(o.shape, BF16) for o in outputs] + [band_sums],
            out_specs + [whole(band_sums)],
        )
        return grads_out, partial, tp_swap(partial, 1)

    def tail_back():
        outs = [struct((1, own_width, p.shape[2]), BF16) for p in projections]
        in_place = capacity % 16 == 0
        outs.append(
            struct((groups, 4 * capacity, own_width) if in_place else (4, slots, own_width), BF16)
        )
        *grads_proj, back = order.call(
            tail_back_kernel,
            in_place,
            "tail_back",
            (part, far, rows, *projections),
            [whole(part), whole(far), whole(rows)] + proj_specs,
            outs,
            [whole(o) for o in outs],
        )
        return grads_proj, back

    def tail_return(back):
        if back.shape[0] != groups or capacity % 16:
            back = back.reshape(4, groups, capacity, own_width).transpose(1, 0, 2, 3)
        returned = lax.all_to_all(
            back.reshape(groups, 4 * capacity, own_width),
            "vocab",
            split_axis=0,
            concat_axis=0,
            tiled=True,
        )
        return returned.reshape(tok_rows, own_width)

    def head_back():
        count = splits // 2
        *own_expd, _ = head_groups[0]

        def part_of(i):
            return jnp.where(i < count, 2 * i + 1, 2 * (i - count))

        pair = struct((count, tok_rows, own_width), BF16)
        give, keep = order.call(
            back_kernel,
            (splits, block, clus_cols),
            "head_back",
            (*own_expd, ids, *early, head_words, clus_padded),
            [whole(v) for v in own_expd]
            + [stat_block] * (1 + splits)
            + [
                pl.BlockSpec((own_width, word_cols), lambda i, s: (s[0] ^ part_of(i), 0)),
                pl.BlockSpec((own_width, LANES), lambda i, s: (s[0] ^ part_of(i), 0)),
            ],
            [pair, pair],
            [
                pl.BlockSpec((1, tok_rows, own_width), lambda i, s: (jnp.minimum(i, count - 1), 0, 0)),
                pl.BlockSpec((1, tok_rows, own_width), lambda i, s: (jnp.maximum(i - count, 0), 0, 0)),
            ],
            [
                pltpu.VMEM((tok_rows, word_cols), BF16),
                pltpu.VMEM((tok_rows, LANES), BF16),
                pltpu.VMEM((tok_rows, LANES), F32),
            ],
            (splits,),
        )
        return keep, tp_swap(give, 1)

    def grad_hidden_step():
        out = struct((tok_rows, own_width), BF16)
        pair = pl.BlockSpec((1, tok_rows, own_width), lambda i, s: (0, 0, 0))
        return order.call(
            final_kernel,
            None,
            "grad_hidden",
            (dispatch, returned, back_keep, back_beside, back_far),
            [whole(dispatch), whole(returned), pair, pair, whole(back_far)],
            out,
            whole(out),
        )

    def weight_grads(first, steps, columns):
        rest = (near - 1) * out_rows
        sizes = tuple(group[0].shape[0] for group in head_groups)
        cols = steps * block + (LANES if columns is not None else 0)
        outs = [struct((out_rows, cols), BF16), struct((rest, cols), BF16)]
        expds, clus, stats, turned = zip(*head_groups)
        operands = [*turned, *expds]
        in_specs = [whole(t) for t in turned]
        in_specs += [pl.BlockSpec((size, block), lambda i, s: (0, i + first)) for size in sizes]
        if columns is None:
            others = other_ids
            extra = [*stats, ids]
            in_specs += [whole(v) for v in extra]
            lanes = []
            at = 0
            for size in sizes[1:]:
                lanes.append(pl.BlockSpec((8, size), lambda i, s, place=at // size: (0, place)))
                at += size
            in_specs += lanes + [stat_block] * splits
            in_specs += [spec for spec in lanes for _ in range(splits)]
            extra += [others] * len(lanes) + early + late * len(lanes)
            outs.append(struct((line * tok_rows, LANES), F32))
        else:
            extra = [columns, *clus]
            in_specs += [whole(v) for v in extra]
        return order.call(
            weights_kernel,
            (splits, quarter, clus_cols, word_cols, sizes, first, columns is not None),
            "head_weights",
            operands + extra,
            in_specs,
            outs,
            [whole(o) for o in outs],
            [pltpu.VMEM((line * tok_rows, block), BF16)],
            (steps,),
        )

    def near_parts(own, rest):
        parts = [own]
        for step in range(1, near):
            part = rest[(step - 1) * out_rows : step * out_rows]
            parts.append(lax.ppermute(part, "vocab", xor_pairs(groups, step)))
        return parts

    def near_sum(parts):
        return sum(part.astype(F32) for part in parts).astype(BF16)

    head_groups = []

    def head_group(*steps, earlier=()):
        *group, mine = head_logits([p for step in steps for p in chunks[step]], earlier)
        head_groups.append(group)
        return mine

    dispatch, send = tail_rows()
    moved_ids = order.hold(*moved_ids)
    (other_ids,) = order.hold(line_ids())
    move_rows(1)
    early = head_group(0)
    early = [early] + shared(early)
    move_rows(2)
    rows, digits = tail_send(*order.hold(send))
    back_keep, back_beside = head_back()
    move_rows(3)
    late = head_group(1, 2)
    (rows,) = order.hold(rows)
    across_rows, beside_rows = tp_swap(rows, 2), tp_swap(rows, 1)
    move_rows(4)
    second = pl.BlockSpec((1, tok_rows, own_width), lambda i, s: (1, 0, 0))
    back_far = added(back_keep, back_beside, [second, second])
    late = head_group(3, earlier=(late,))
    late = [late] + shared(late)
    (across_rows,) = order.hold(across_rows)
    back_far = tp_swap(back_far, 2)
    all_rows = [rows, beside_rows, across_rows, tp_swap(across_rows, 1)]
    reduced, tail_expd, tail_stats = tail_logits()
    tail_shares = shared(tail_stats)
    (back_far,) = order.hold(back_far)
    grads_out, part, beside = tail_grads()
    part = added(part, beside)
    far = tp_swap(part, 2)
    ahead = blocks - 1
    *first_parts, columns = weight_grads(0, ahead, None)
    first_sum = near_parts(*first_parts)
    grads_proj, back = tail_back()
    returned = tail_return(back)
    second_sum = near_parts(*weight_grads(ahead, blocks - ahead, columns))
    grad_hidden = grad_hidden_step()
    second_sum = near_sum(order.hold(*second_sum))
    at = (blocks - ahead) * block
    sums = [near_sum(first_sum), second_sum[:, :at]]
    clus_sum = second_sum[:, at : at + clus_cols]
    return (
        grad_hidden,
        jnp.concatenate(sums, axis=1),
        clus_sum,
        *grads_proj,
        *grads_out,
    )


def solution(mesh):
    return jax.shard_map(
        body,
        mesh=mesh,
        in_specs=(
            P("vocab", None),
            P("vocab", None),
            P("vocab"),
            P(None, "tp"),
            P(None, "tp"),
            P("vocab", None, None),
            P("vocab", None, None),
            P("vocab", None, None),
            P("vocab", None, None),
            P("vocab", None, "tp"),
            P("vocab", None, "tp"),
            P("vocab", None, "tp"),
            P("vocab", None, "tp"),
        ),
        out_specs=(
            P("vocab", "tp"),
            P("vocab", "tp"),
            P("vocab", "tp"),
            P("vocab", "tp", None),
            P("vocab", "tp", None),
            P("vocab", "tp", None),
            P("vocab", "tp", None),
            P("vocab", None, "tp"),
            P("vocab", None, "tp"),
            P("vocab", None, "tp"),
            P("vocab", None, "tp"),
        ),
        check_vma=False,
    )
```
